256 devices in a mesh: dp: 16 (over z, y_hi), tensor: 16 (over x, y_lo, core).
Axes of the slice: x: 4, y: 4 (y_hi: 2, y_lo: 2; y = y_hi * 2 + y_lo), z: 8, core: 2. Of those that a mesh axis runs over, the one named last changes fastest.
Arguments:
- inputs: bfloat16 [2048, 16384], P('tensor', 'dp'), may hold values from -6 to 6
- out_grad: bfloat16 [2048, 16384], P('tensor', 'dp'), may hold values from -6 to 6
- attn_out: bfloat16 [2048, 12288], P('dp', 'tensor'), may hold values from -6 to 6
- qkv_grad: bfloat16 [2048, 14336], P('dp', 'tensor'), may hold values from -6 to 6
- w_qkv: bfloat16 [16384, 14336], P('dp', 'tensor'), may hold values from -0.046875 to 0.046875
- w_out: bfloat16 [12288, 16384], P('tensor', 'dp'), may hold values from -0.0546875 to 0.0546875
- doc_ids: int32 [2048], P('dp'), may hold values from 0 to 15, as said below
Outputs:
- input_grad: bfloat16 [2048, 16384], P('tensor', 'dp')
- attn_grad: bfloat16 [2048, 12288], P('dp', 'tensor')
- wqkv_grad: float32 [16384, 14336], P('dp', 'tensor')
- wout_grad: float32 [12288, 16384], P('tensor', 'dp')
The draws below stay inside these ranges and needn't reach their ends.
Inputs may be any that keep to these rules, and one draw needn't show every extreme that they name: `doc_ids`: ids never fall along the tokens; every id occurs; each document holds 1 to 960 tokens; document 0 holds fewer than 128 tokens and the last document holds exactly 960.
All inputs are finite; a program needn't handle non-finite values.
Results may differ from the reference program's by a relative error of at most 0.019.
Values may be sent and summed in bfloat16 or wider, within the bound.
No kernel may reach another device: no remote copies, remote signals or barrier semaphores. Data moves between devices by JAX's collectives and lax.ppermute only.
A program may use at most 128 MiB of HBM per device.

```python
import math
import jax
import jax.numpy as jnp
from jax import lax

D = 16384
HD = 128
HQ = 96
HK = 8
TOK_DEV = 128
TOKENS = 2048
QKV = 14336
ROWS_O = 12288
DOCS = 16
MOST = 960
N_DP = 16
N_TENSOR = 16


def draw_doc_ids(key, part):
    key = jax.random.fold_in(key, 11)
    first_key, cut_key = jax.random.split(key)
    first_len = jax.random.randint(first_key, (), 1, TOK_DEV, dtype=jnp.int32)
    spare = TOKENS // 2 - TOK_DEV // 2 + 1
    half = spare // 2
    picked = jax.random.permutation(cut_key, spare - 2)[:DOCS - 4].astype(jnp.int32) + 1
    picked = jnp.where(picked >= half, picked + 1, picked)
    cuts = jnp.concatenate([picked, jnp.full((1,), half, jnp.int32)])
    token_index = jnp.arange(TOKENS, dtype=jnp.int32)
    offset = token_index - first_len
    middle = 1 + jnp.sum((cuts[None, :] <= offset[:, None]).astype(jnp.int32), axis=1)
    last_start = TOKENS - MOST
    return jnp.where(token_index < first_len, 0, jnp.where(token_index >= last_start, DOCS - 1, middle)).astype(jnp.int32)


def block_scale(stream_key, shape, cuts, low, largest):
    gain, own = 1.0, jax.random.fold_in(stream_key, 6)
    for dim, shards_of in cuts:
        draws = jnp.exp(jax.random.uniform(jax.random.fold_in(own, dim), (shards_of,), jnp.float32, low / len(cuts), largest / len(cuts)))
        gain = gain * jnp.repeat(draws, shape[dim] // shards_of).reshape([-1 if axis == dim else 1 for axis in range(len(shape))])
    return gain


def normal_values(own_key, dims, spread, limit, cuts=(), kind=jnp.bfloat16):
    result = jax.random.normal(own_key, dims, jnp.float32) * spread
    if len(cuts) > 0:
        result = block_scale(own_key, dims, cuts, -0.22, 0.18) * result
    return jnp.clip(result, min=-limit, max=limit).astype(kind)


def setup_inputs(seed: int = 0) -> dict:
    key_of = jax.random.split(jax.random.key(seed), 8)
    inputs = normal_values(key_of[0], (TOKENS, D), 1.0, 6.0, ((0, 16), (1, 16)))
    out_grad = normal_values(key_of[1], (TOKENS, D), 1.0, 6.0, ((0, 16), (1, 16)))
    attn_out = normal_values(key_of[2], (TOKENS, ROWS_O), 1.0, 6.0, ((0, 16), (1, 16)))
    qkv_grad = normal_values(key_of[3], (TOKENS, QKV), 1.0, 6.0, ((0, 16), (1, 16)))
    w_qkv = normal_values(key_of[4], (D, QKV), D ** -0.5, 0.046875, ((0, 16), (1, 16)))
    w_out = normal_values(key_of[5], (ROWS_O, D), ROWS_O ** -0.5, 0.0546875, ((0, 16), (1, 16)))
    doc_ids = draw_doc_ids(jax.random.fold_in(key_of[7], 71), 0)
    return {"inputs": inputs, "out_grad": out_grad, "attn_out": attn_out, "qkv_grad": qkv_grad, "w_qkv": w_qkv, "w_out": w_out, "doc_ids": doc_ids}


ROPE_BASE = 500000.0

def positions_of(doc_ids):
    length = doc_ids.shape[0]
    token_index = jnp.arange(length, dtype=jnp.int32)
    boundary = jnp.concatenate([jnp.ones((1,), bool), doc_ids[1:] != doc_ids[:-1]])
    starts_here = jnp.where(boundary, token_index, 0).astype(jnp.int32)
    return (token_index - lax.cummax(starts_here, axis=0)).astype(jnp.int32)

def unrotate(gradient, positions, columns):
    pair_index = columns % HD // 2
    frequency = jnp.power(jnp.float32(ROPE_BASE), -(2.0 * pair_index.astype(jnp.float32)) / HD)
    rotated = columns < (HQ + HK) * HD
    angles = positions.astype(jnp.float32)[:, None] * frequency[None, :]
    cosine_part = jnp.where(rotated[None, :], jnp.cos(angles), 1.0)
    sine_part = jnp.where(rotated[None, :], jnp.sin(angles), 0.0)
    is_even = columns % 2 == 0
    values = gradient.astype(jnp.float32)
    partner = jnp.where(is_even[None, :], jnp.roll(values, -1, axis=1), jnp.roll(values, 1, axis=1))
    flip_sign = jnp.where(is_even, 1.0, -1.0)
    return (values * cosine_part + partner * flip_sign[None, :] * sine_part).astype(jnp.bfloat16)

def rounded(term):
    return lax.optimization_barrier(term.astype(jnp.bfloat16)).astype(jnp.float32)

def reference(inputs, out_grad, attn_out, qkv_grad, w_qkv, w_out, doc_ids):
    positions = positions_of(doc_ids)
    columns = jnp.arange(QKV, dtype=jnp.int32)
    pre_rope = unrotate(qkv_grad, positions, columns)
    factor = 1.0 / math.sqrt(TOKENS)
    wqkv_grad = jnp.dot(inputs.T, pre_rope, preferred_element_type=jnp.float32) * factor
    wout_grad = jnp.dot(attn_out.T, out_grad, preferred_element_type=jnp.float32) * factor
    block_cols = QKV // N_TENSOR
    block_width = D // N_DP

    def input_block(block, total):
        start = (block * block_cols).astype(jnp.int32)
        grads_part = lax.dynamic_slice_in_dim(pre_rope, start, block_cols, 1)
        weight_part = lax.dynamic_slice_in_dim(w_qkv, start, block_cols, 1)
        term = lax.dot_general(grads_part, weight_part, (((1,), (1,)), ((), ())), preferred_element_type=jnp.float32)
        return total + rounded(term)
    summed = lax.fori_loop(0, N_TENSOR, input_block, jnp.zeros((TOKENS, D), jnp.float32))
    input_grad = (out_grad.astype(jnp.float32) + summed).astype(jnp.bfloat16)

    def attn_block(block, total):
        start = (block * block_width).astype(jnp.int32)
        grads_part = lax.dynamic_slice_in_dim(out_grad, start, block_width, 1)
        weight_part = lax.dynamic_slice_in_dim(w_out, start, block_width, 1)
        term = lax.dot_general(grads_part, weight_part, (((1,), (1,)), ((), ())), preferred_element_type=jnp.float32)
        return total + rounded(term)
    attn_sum = lax.fori_loop(0, N_DP, attn_block, jnp.zeros((TOKENS, ROWS_O), jnp.float32))
    attn_grad = attn_sum.astype(jnp.bfloat16)
    return (input_grad, attn_grad, wqkv_grad, wout_grad)
```

```python
import math

import jax
import jax.numpy as jnp
from jax import lax
from jax.sharding import PartitionSpec as P

HD = 128
HQ = 96
HK = 8
ROPE_BASE = 500000.0
NZ = 8
NX = 4
TB = 128


def over_z(value, steps):
    pairs = [(z * 2 + h, (z + steps) % NZ * 2 + h) for z in range(NZ) for h in range(2)]
    return lax.ppermute(value, "dp", pairs)


def over_yh(value):
    return lax.ppermute(value, "dp", [(d, d ^ 1) for d in range(16)])


def over_x(value, steps):
    pairs = [(x * 4 + k, (x + steps) % NX * 4 + k) for x in range(NX) for k in range(4)]
    return lax.ppermute(value, "tensor", pairs)


def over_yl(value):
    return lax.ppermute(value, "tensor", [(t, t ^ 2) for t in range(16)])


def over_core(value):
    return lax.ppermute(value, "tensor", [(t, t ^ 1) for t in range(16)])


def local_positions(doc_ids, all_ids):
    token_index = lax.axis_index("dp") * TB + jnp.arange(TB, dtype=jnp.int32)
    smaller = (all_ids[None, :] < doc_ids[:, None]).astype(jnp.int32)
    return token_index - jnp.sum(smaller, axis=1)


def unrotate(gradient, positions, columns):
    pair_index = jnp.arange(HD, dtype=jnp.int32) // 2
    frequency = jnp.power(jnp.float32(ROPE_BASE), -(2.0 * pair_index.astype(jnp.float32)) / HD)
    angles = positions.astype(jnp.float32)[:, None] * frequency[None, :]
    heads = gradient.shape[1] // HD
    cosine = jnp.tile(jnp.cos(angles), (1, heads))
    sine = jnp.tile(jnp.sin(angles), (1, heads))
    rotated = columns < (HQ + HK) * HD
    cosine_part = jnp.where(rotated[None, :], cosine, 1.0)
    sine_part = jnp.where(rotated[None, :], sine, 0.0)
    is_even = columns % 2 == 0
    values = gradient.astype(jnp.float32)
    partner = jnp.where(is_even[None, :], jnp.roll(values, -1, axis=1), jnp.roll(values, 1, axis=1))
    flip_sign = jnp.where(is_even, 1.0, -1.0)
    return (values * cosine_part + partner * flip_sign[None, :] * sine_part).astype(jnp.bfloat16)


def contract_rows(left, right):
    return lax.dot_general(
        left, right, (((0,), (0,)), ((), ())), preferred_element_type=jnp.float32
    )


def contract_cols(left, right):
    return lax.dot_general(
        left, right, (((1,), (1,)), ((), ())), preferred_element_type=jnp.float32
    )


def ordered_pair(own, other, second):
    return jnp.where(second, jnp.concatenate([other, own]), jnp.concatenate([own, other]))


def gather_z(block, z, yh, long_way):
    pair = ordered_pair(block, over_yh(block), yh == 1)
    rows = pair.shape[0]
    whole = jnp.zeros((NZ * rows, block.shape[1]), block.dtype)
    put = lambda whole, part, at: lax.dynamic_update_slice_in_dim(whole, part, at % NZ * rows, 0)
    whole = put(whole, pair, z)
    up = down = pair
    for k in range(1, 5):
        if k < 4 or long_way > 0:
            up = over_z(up, 1)
            whole = put(whole, up, z - k + NZ)
        if k < 4 or long_way < 0:
            down = over_z(down, -1)
            whole = put(whole, down, z + k)
    return whole


def scatter_z(partial, z, long_way):
    rows = 2 * TB
    mine = lambda at: lax.dynamic_slice_in_dim(partial, at % NZ * rows, rows, 0).astype(jnp.float32)
    up = down = None
    for k in range(4, 0, -1):
        if k < 4 or long_way > 0:
            part = mine(z + k)
            up = over_z((part if up is None else part + up.astype(jnp.float32)).astype(jnp.bfloat16), 1)
        if k < 4 or long_way < 0:
            part = mine(z - k + NZ)
            down = over_z((part if down is None else part + down.astype(jnp.float32)).astype(jnp.bfloat16), -1)
    return mine(z) + up.astype(jnp.float32) + down.astype(jnp.float32)


def shards(inputs, out_grad, attn_out, qkv_grad, w_qkv, w_out, doc_ids):
    d, t = lax.axis_index("dp"), lax.axis_index("tensor")
    z, yh = d // 2, d % 2
    x, yl, core = t // 4, t // 2 % 2, t % 2
    shard_cols = qkv_grad.shape[1]
    columns = t * shard_cols + jnp.arange(shard_cols, dtype=jnp.int32)

    all_ids = lax.all_gather(doc_ids, "dp", axis=0, tiled=True)
    g_all = lax.all_gather(out_grad, "tensor", axis=0, tiled=True)
    x_all = lax.all_gather(inputs, "tensor", axis=0, tiled=True)

    a_all = gather_z(attn_out, z, yh, 1)
    pre_rope = unrotate(qkv_grad, local_positions(doc_ids, all_ids), columns)
    q_all = gather_z(pre_rope, z, yh, -1)

    factor = 1.0 / math.sqrt(g_all.shape[0])
    attn_part = contract_cols(g_all, w_out).astype(jnp.bfloat16)
    half = attn_part.shape[1] // 2
    sums = jnp.concatenate(
        [scatter_z(attn_part[:, :half], z, 1), scatter_z(attn_part[:, half:], z, -1)], axis=1
    )
    keep = lax.dynamic_slice_in_dim(sums, yh * TB, TB, 0)
    give = lax.dynamic_slice_in_dim(sums, (1 - yh) * TB, TB, 0).astype(jnp.bfloat16)
    attn_grad = (keep + over_yh(give).astype(jnp.float32)).astype(jnp.bfloat16)

    q_blocks = q_all.reshape(8, 2, TB, shard_cols)
    of_core = lambda c: lax.dynamic_index_in_dim(q_blocks, c, 1, False).reshape(8 * TB, shard_cols)
    sent = over_core(contract_cols(of_core(1 - core), w_qkv).astype(jnp.bfloat16))
    chip = contract_cols(of_core(core), w_qkv) + sent.astype(jnp.float32)
    chip = chip.astype(jnp.bfloat16)
    toward = lambda at: lax.dynamic_slice_in_dim(chip, at % NX * 2 * TB, 2 * TB, 0)
    total = toward(x).astype(jnp.float32)
    for steps in (1, -1, 2):
        total = total + over_x(toward(x + steps + NX), steps).astype(jnp.float32)
    keep = lax.dynamic_slice_in_dim(total, yl * TB, TB, 0)
    give = lax.dynamic_slice_in_dim(total, (1 - yl) * TB, TB, 0).astype(jnp.bfloat16)
    summed = keep + over_yl(give).astype(jnp.float32)
    input_grad = (out_grad.astype(jnp.float32) + summed).astype(jnp.bfloat16)

    wout_grad = contract_rows(a_all, g_all) * factor
    wqkv_grad = contract_rows(x_all, q_all) * factor
    return (input_grad, attn_grad, wqkv_grad, wout_grad)


def solution(mesh):
    return jax.shard_map(
        shards,
        mesh=mesh,
        in_specs=(
            P("tensor", "dp"),
            P("tensor", "dp"),
            P("dp", "tensor"),
            P("dp", "tensor"),
            P("dp", "tensor"),
            P("tensor", "dp"),
            P("dp"),
        ),
        out_specs=(P("tensor", "dp"), P("dp", "tensor"), P("dp", "tensor"), P("tensor", "dp")),
        check_vma=False,
    )
```

```python
import math

import jax
import jax.numpy as jnp
from jax import lax
from jax.experimental import pallas as pl
from jax.experimental.pallas import tpu as pltpu
from jax.sharding import PartitionSpec as P

HD = 128
HQ = 96
HK = 8
ROPE_BASE = 500000.0
NZ = 8
NX = 4
TB = 128
BEHIND = 5


def over_z(value, steps):
    pairs = [(z * 2 + h, (z + steps) % NZ * 2 + h) for z in range(NZ) for h in range(2)]
    return lax.ppermute(value, "dp", pairs)


def over_yh(value):
    return lax.ppermute(value, "dp", [(d, d ^ 1) for d in range(16)])


def over_x(value, steps):
    pairs = [(x * 4 + k, (x + steps) % NX * 4 + k) for x in range(NX) for k in range(4)]
    return lax.ppermute(value, "tensor", pairs)


def over_yl(value):
    return lax.ppermute(value, "tensor", [(t, t ^ 2) for t in range(16)])


def over_core(value):
    return lax.ppermute(value, "tensor", [(t, t ^ 1) for t in range(16)])


def after(value, *earlier):
    return lax.optimization_barrier((value, *earlier))[0]


def local_positions(doc_ids, z, yh):
    ids = doc_ids[None, :]
    other = over_yh(ids)
    pair = jnp.where(yh == 1, jnp.concatenate([other, ids]), jnp.concatenate([ids, other]))
    one, two = over_z(pair, 1), over_z(pair, 2)
    far = over_z(jnp.concatenate([two, one, pair]), 3)
    window = jnp.concatenate([far, two, one, pair]).reshape(-1)
    smaller = jnp.sum((window[None, :] < doc_ids[:, None]).astype(jnp.int32), axis=1)
    start = jnp.maximum((z - BEHIND) * 2 * TB, 0) + smaller
    return z * 2 * TB + yh * TB + jnp.arange(TB, dtype=jnp.int32) - start


def unrotate_kernel(first_ref, g_ref, cos_ref, sin_ref, out_ref):
    even = lax.broadcasted_iota(jnp.int32, (TB, HD), 1) % 2 == 0
    for h in range(g_ref.shape[1] // HD):
        rotated = first_ref[0] + h < HQ + HK
        values = g_ref[:, h * HD : (h + 1) * HD].astype(jnp.float32)
        partner = jnp.where(even, pltpu.roll(values, HD - 1, 1), pltpu.roll(values, 1, 1))
        cosine = jnp.where(rotated, cos_ref[...], 1.0)
        sine = jnp.where(rotated, sin_ref[...], 0.0)
        out_ref[:, h * HD : (h + 1) * HD] = (values * cosine + partner * sine).astype(jnp.bfloat16)


def unrotate(gradient, positions, t):
    lane = jnp.arange(HD, dtype=jnp.int32)
    frequency = jnp.power(jnp.float32(ROPE_BASE), -(2.0 * (lane // 2).astype(jnp.float32)) / HD)
    angles = positions.astype(jnp.float32)[:, None] * frequency[None, :]
    sign = jnp.where(lane % 2 == 0, 1.0, -1.0)
    first_head = jnp.reshape(t * (gradient.shape[1] // HD), (1,)).astype(jnp.int32)
    vmem = pl.BlockSpec(memory_space=pltpu.VMEM)
    return pl.pallas_call(
        unrotate_kernel,
        out_shape=jax.ShapeDtypeStruct(gradient.shape, jnp.bfloat16),
        in_specs=[pl.BlockSpec(memory_space=pltpu.SMEM), vmem, vmem, vmem],
        out_specs=vmem,
    )(first_head, gradient, jnp.cos(angles), jnp.sin(angles) * sign[None, :])


def rows_kernel(factor, split_left, yh_ref, own_ref, other_ref, both_ref, out_ref):
    yh = yh_ref[0]
    total = jnp.zeros(out_ref.shape, jnp.float32)
    for part, h in ((own_ref, yh), (other_ref, 1 - yh)):
        tokens = both_ref[:, h].reshape(NZ * TB, both_ref.shape[-1])
        left, right = (part[...], tokens) if split_left else (tokens, part[...])
        total += lax.dot_general(left, right, (((0,), (0,)), ((), ())), preferred_element_type=jnp.float32)
    out_ref[...] = total * factor


def contract_rows(own, other, both, yh, factor, split_left, tile):
    tokens, a = own.shape
    b = both.shape[1]
    if split_left:
        m, n = a, b
        pair = pl.BlockSpec((tokens, tile), lambda i, _: (0, i))
        whole = pl.BlockSpec((NZ, 2, TB, b), lambda i, _: (0, 0, 0, 0))
    else:
        m, n = b, a
        pair = pl.BlockSpec((tokens, a), lambda i, _: (0, 0))
        whole = pl.BlockSpec((NZ, 2, TB, tile), lambda i, _: (0, 0, 0, i))
    return pl.pallas_call(
        lambda *refs: rows_kernel(factor, split_left, *refs),
        out_shape=jax.ShapeDtypeStruct((m, n), jnp.float32),
        grid_spec=pltpu.PrefetchScalarGridSpec(
            num_scalar_prefetch=1,
            grid=(m // tile,),
            in_specs=[pair, pair, whole],
            out_specs=pl.BlockSpec((tile, n), lambda i, _: (i, 0)),
        ),
        compiler_params=pltpu.CompilerParams(vmem_limit_bytes=40 * 2**20),
        cost_estimate=pl.CostEstimate(
            flops=4 * tokens * a * b, bytes_accessed=4 * tokens * (a + b) + 4 * a * b, transcendentals=0
        ),
    )(jnp.reshape(yh, (1,)).astype(jnp.int32), own, other, both.reshape(NZ, 2, TB, b))


def contract_cols(left, right):
    return lax.dot_general(
        left, right, (((1,), (1,)), ((), ())), preferred_element_type=jnp.float32
    )


class Ring:
    def __init__(self, block, z, long_way):
        self.up = self.down = block
        self.z, self.long_way, self.k = z, long_way, 0
        self.whole = jnp.zeros((NZ * TB, block.shape[1]), block.dtype)
        self.put(block, z)

    def put(self, part, at):
        self.whole = lax.dynamic_update_slice_in_dim(self.whole, part, at % NZ * TB, 0)

    def step(self, *earlier):
        self.k += 1
        k = self.k
        up, down = self.up, self.down
        if earlier:
            up, down = lax.optimization_barrier((up, down, *earlier))[:2]
        if k < 4 or self.long_way > 0:
            self.up = over_z(up, 1)
            self.put(self.up, self.z - k + NZ)
        if k < 4 or self.long_way < 0:
            self.down = over_z(down, -1)
            self.put(self.down, self.z + k)

    @property
    def last(self):
        return (self.up, self.down)


class Fold:
    def __init__(self, partial, z, long_way):
        self.partial, self.z, self.long_way, self.k = partial, z, long_way, 4
        self.rows = partial.shape[0] // NZ
        self.up = self.down = None

    def mine(self, at):
        return lax.dynamic_slice_in_dim(self.partial, at % NZ * self.rows, self.rows, 0).astype(jnp.float32)

    def add(self, part, got):
        return (part if got is None else part + got.astype(jnp.float32)).astype(jnp.bfloat16)

    def step(self, *earlier):
        k = self.k
        self.k -= 1
        up = down = None
        if k < 4 or self.long_way > 0:
            up = self.add(self.mine(self.z + k), self.up)
        if k < 4 or self.long_way < 0:
            down = self.add(self.mine(self.z - k + NZ), self.down)
        if earlier:
            up, down = lax.optimization_barrier((up, down, *earlier))[:2]
        if up is not None:
            self.up = over_z(up, 1)
        if down is not None:
            self.down = over_z(down, -1)

    @property
    def last(self):
        return tuple(v for v in (self.up, self.down) if v is not None)

    def sums(self):
        return self.mine(self.z) + self.up.astype(jnp.float32) + self.down.astype(jnp.float32)


def shards(inputs, out_grad, attn_out, qkv_grad, w_qkv, w_out, doc_ids):
    d, t = lax.axis_index("dp"), lax.axis_index("tensor")
    z, yh = d // 2, d % 2
    x, yl, core = t // 4, t // 2 % 2, t % 2
    cols = qkv_grad.shape[1]
    factor = 1.0 / math.sqrt(NZ * 2 * TB)

    g_all = lax.all_gather(out_grad, "tensor", axis=0, tiled=True)
    x_all = lax.all_gather(inputs, "tensor", axis=0, tiled=True)

    a = Ring(attn_out, z, 1)
    a.step()
    a.step()
    pre_rope = unrotate(qkv_grad, local_positions(doc_ids, z, yh), t)
    qo = Ring(pre_rope, z, -1)
    qp = Ring(over_yh(pre_rope), z, 1)
    qo.step(*a.last)
    a.step()
    qp.step()
    a.step()
    qo.step()
    qp.step(*a.last)
    a_other = over_yh(a.whole)

    attn_part = contract_cols(g_all, w_out).astype(jnp.bfloat16)
    half = attn_part.shape[1] // 2

    qo.step(attn_part)
    qp.step()
    qo.step()
    qp.step()
    q_own, q_other = qo.whole, qp.whole

    r1 = Fold(attn_part[:, :half], z, -1)
    blocks = attn_part.reshape(NZ, 2, TB, 2 * half)[..., half:]
    pick = lambda h: lax.dynamic_index_in_dim(blocks, h, 1, False).reshape(NZ * TB, half)
    swapped = over_yh(after(pick(1 - yh), *qo.last))
    r1.step(*qo.last)
    r1.step(*qp.last)
    r2 = Fold((pick(yh).astype(jnp.float32) + swapped.astype(jnp.float32)).astype(jnp.bfloat16), z, 1)
    r2.step(*r1.last)
    r1.step()
    r2.step()
    r1.step(a_other)
    r2.step()
    r2.step()
    sums = r1.sums()
    keep = lax.dynamic_slice_in_dim(sums, yh * TB, TB, 0)
    give = lax.dynamic_slice_in_dim(sums, (1 - yh) * TB, TB, 0).astype(jnp.bfloat16)
    attn_grad = jnp.concatenate([keep + over_yh(give).astype(jnp.float32), r2.sums()], axis=1).astype(
        jnp.bfloat16
    )

    q_of = lambda c: jnp.where(c == yh, q_own, q_other)
    sent = over_core(contract_cols(q_of(1 - core), w_qkv).astype(jnp.bfloat16))
    chip = contract_cols(q_of(core), w_qkv) + sent.astype(jnp.float32)
    chip = chip.astype(jnp.bfloat16)
    toward = lambda at: lax.dynamic_slice_in_dim(chip, at % NX * 2 * TB, 2 * TB, 0)
    total = toward(x).astype(jnp.float32)
    for steps in (1, -1, 2):
        total = total + over_x(toward(x + steps + NX), steps).astype(jnp.float32)
    keep = lax.dynamic_slice_in_dim(total, yl * TB, TB, 0)
    give = lax.dynamic_slice_in_dim(total, (1 - yl) * TB, TB, 0).astype(jnp.bfloat16)
    summed = keep + over_yl(give).astype(jnp.float32)
    input_grad = (out_grad.astype(jnp.float32) + summed).astype(jnp.bfloat16)

    wout_grad = contract_rows(a.whole, a_other, g_all, yh, factor, True, 256)
    wqkv_grad = contract_rows(q_own, q_other, x_all, yh, factor, False, 256)
    return (input_grad, attn_grad, wqkv_grad, wout_grad)


def solution(mesh):
    return jax.shard_map(
        shards,
        mesh=mesh,
        in_specs=(
            P("tensor", "dp"),
            P("tensor", "dp"),
            P("dp", "tensor"),
            P("dp", "tensor"),
            P("dp", "tensor"),
            P("tensor", "dp"),
            P("dp"),
        ),
        out_specs=(P("tensor", "dp"), P("dp", "tensor"), P("dp", "tensor"), P("tensor", "dp")),
        check_vma=False,
    )
```

```python
import math

import jax
import jax.numpy as jnp
from jax import lax
from jax.experimental import pallas as pl
from jax.experimental.pallas import tpu as pltpu
from jax.sharding import PartitionSpec as P

HD = 128
HQ = 96
HK = 8
ROPE_BASE = 500000.0
NZ = 8
NX = 4
TB = 128
DOCS = 16


def over_z(value, steps):
    pairs = [(z * 2 + h, (z + steps) % NZ * 2 + h) for z in range(NZ) for h in range(2)]
    return lax.ppermute(value, "dp", pairs)


def over_yh(value):
    return lax.ppermute(value, "dp", [(d, d ^ 1) for d in range(16)])


def over_x(value, steps):
    pairs = [(x * 4 + k, (x + steps) % NX * 4 + k) for x in range(NX) for k in range(4)]
    return lax.ppermute(value, "tensor", pairs)


def over_yl(value):
    return lax.ppermute(value, "tensor", [(t, t ^ 2) for t in range(16)])


def over_core(value):
    return lax.ppermute(value, "tensor", [(t, t ^ 1) for t in range(16)])


def tie(*values):
    return lax.optimization_barrier(values)


def in_token_order(window, z):
    twice = jnp.concatenate([window, window])
    return lax.dynamic_slice_in_dim(twice, (NZ - 1 - z) * 2, 2 * NZ, 0).reshape(-1)


def rotary_tables(ids):
    labels = jnp.arange(DOCS, dtype=jnp.int32)
    starts = jnp.sum((ids[None, :] < labels[:, None]).astype(jnp.int32), axis=1)
    start = jnp.sum(jnp.where(ids[:, None] == labels[None, :], starts[None, :], 0), axis=1)
    positions = jnp.arange(ids.shape[0], dtype=jnp.int32) - start
    lane = jnp.arange(HD, dtype=jnp.int32)
    frequency = jnp.power(jnp.float32(ROPE_BASE), -(2.0 * (lane // 2).astype(jnp.float32)) / HD)
    angles = positions.astype(jnp.float32)[:, None] * frequency[None, :]
    sign = jnp.where(lane % 2 == 0, 1.0, -1.0)
    return jnp.cos(angles), jnp.sin(angles) * sign[None, :]


def unrotate_kernel(count, heads, where_ref, *refs):
    own, other = refs[:count], refs[count : 2 * count]
    cos_own, sin_own, cos_other, sin_other = refs[2 * count : 2 * count + 4]
    own_out, other_out, attn_out = refs[-3:]
    even = lax.broadcasted_iota(jnp.int32, (TB, HD), 1) % 2 == 0
    first = pl.program_id(0) == 0

    def landed(blocks, part):
        return blocks[0][:, part] if count == 1 else jnp.where(first, blocks[0][:, part], blocks[1][:, part])

    attn_cols = attn_out.shape[1]
    attn_out[...] = landed(own, slice(0, attn_cols))
    for blocks, skip, cos_ref, sin_ref, out_ref in (
        (own, attn_cols, cos_own, sin_own, own_out),
        (other, 0, cos_other, sin_other, other_out),
    ):
        for h in range(heads):
            rotated = where_ref[4 * count] + h < HQ + HK
            values = landed(blocks, slice(skip + h * HD, skip + (h + 1) * HD)).astype(jnp.float32)
            partner = jnp.where(even, pltpu.roll(values, HD - 1, 1), pltpu.roll(values, 1, 1))
            cosine = jnp.where(rotated, cos_ref[...], 1.0)
            sine = jnp.where(rotated, sin_ref[...], 0.0)
            out_ref[:, h * HD : (h + 1) * HD] = (values * cosine + partner * sine).astype(jnp.bfloat16)


def unrotate(own, other, places, z_yh_t, tables, wholes):
    z, yh, t = z_yh_t
    count = len(own)
    cols = other[0].shape[1]
    attn_cols = own[0].shape[1] - cols
    at = [(z + p + NZ) % NZ for p in places]
    where = [*at, *at, *(p * 2 + yh for p in at), *(p * 2 + 1 - yh for p in at), t * (cols // HD)]
    where = jnp.stack(where).astype(jnp.int32)
    mine = pl.BlockSpec((TB, HD), lambda i, s: (s[2 * count + i], 0))
    theirs = pl.BlockSpec((TB, HD), lambda i, s: (s[3 * count + i], 0))
    operands = [*own, *other, tables[0], tables[1], tables[0], tables[1]]
    in_specs = [pl.BlockSpec(v.shape, lambda i, s: (0, 0)) for v in (*own, *other)] + [mine, mine, theirs, theirs]
    aliases = {}
    if wholes is not None:
        aliases = {1 + len(operands) + k: k for k in range(3)}
        operands += wholes
        in_specs += [pl.BlockSpec(memory_space=pl.ANY)] * 3

    def body(where_ref, *refs):
        unrotate_kernel(count, cols // HD, where_ref, *refs[: 2 * count + 4], *refs[-3:])

    widths = (cols, cols, attn_cols)
    return pl.pallas_call(
        body,
        out_shape=tuple(jax.ShapeDtypeStruct((NZ * TB, n), jnp.bfloat16) for n in widths),
        grid_spec=pltpu.PrefetchScalarGridSpec(
            num_scalar_prefetch=1,
            grid=(count,),
            in_specs=in_specs,
            out_specs=tuple(pl.BlockSpec((TB, n), lambda i, s: (s[i], 0)) for n in widths),
        ),
        input_output_aliases=aliases,
        cost_estimate=pl.CostEstimate(
            flops=20 * count * TB * cols, bytes_accessed=8 * count * TB * cols, transcendentals=0
        ),
    )(where, *operands)


def rows_kernel(factor, split_left, where_ref, own_ref, other_ref, both_ref, out_ref):
    yh = where_ref[0]
    total = jnp.zeros(out_ref.shape, jnp.float32)
    for part, h in ((own_ref, yh), (other_ref, 1 - yh)):
        tokens = both_ref[:, h].reshape(NZ * TB, both_ref.shape[-1])
        left, right = (part[...], tokens) if split_left else (tokens, part[...])
        total += lax.dot_general(left, right, (((0,), (0,)), ((), ())), preferred_element_type=jnp.float32)
    out_ref[...] = total * factor


def contract_rows(own, other, both, yh, factor, split_left, tile):
    tokens, a = own.shape
    b = both.shape[1]
    if split_left:
        m, n = a, b
        pair = pl.BlockSpec((tokens, tile), lambda i, _: (0, i))
        whole = pl.BlockSpec((NZ, 2, TB, b), lambda i, _: (0, 0, 0, 0))
    else:
        m, n = b, a
        pair = pl.BlockSpec((tokens, a), lambda i, _: (0, 0))
        whole = pl.BlockSpec((NZ, 2, TB, tile), lambda i, _: (0, 0, 0, i))
    return pl.pallas_call(
        lambda *refs: rows_kernel(factor, split_left, *refs),
        out_shape=jax.ShapeDtypeStruct((m, n), jnp.float32),
        grid_spec=pltpu.PrefetchScalarGridSpec(
            num_scalar_prefetch=1,
            grid=(m // tile,),
            in_specs=[pair, pair, whole],
            out_specs=pl.BlockSpec((tile, n), lambda i, _: (i, 0)),
        ),
        compiler_params=pltpu.CompilerParams(vmem_limit_bytes=40 * 2**20),
        cost_estimate=pl.CostEstimate(
            flops=4 * tokens * a * b, bytes_accessed=4 * tokens * (a + b) + 4 * a * b, transcendentals=0
        ),
    )(jnp.reshape(yh, (1,)).astype(jnp.int32), own, other, both.reshape(NZ, 2, TB, b))


def contract_cols(left, right):
    return lax.dot_general(
        left, right, (((1,), (1,)), ((), ())), preferred_element_type=jnp.float32
    )


class Fold:
    def __init__(self, partial, z):
        self.partial, self.z = partial, z
        self.rows = partial.shape[0] // NZ
        self.up = self.down = None
        self.k = 4

    def mine(self, at):
        return lax.dynamic_slice_in_dim(self.partial, at % NZ * self.rows, self.rows, 0).astype(jnp.float32)

    def add(self, part, got):
        return (part if got is None else part + got.astype(jnp.float32)).astype(jnp.bfloat16)

    def step(self):
        k = self.k
        self.k -= 1
        self.up = over_z(self.add(self.mine(self.z + k), self.up), 1)
        if k > 1:
            self.down = over_z(self.add(self.mine(self.z - k + 1 + NZ), self.down), -1)

    def sums(self):
        return self.mine(self.z) + self.up.astype(jnp.float32) + self.down.astype(jnp.float32)


def shards(inputs, out_grad, attn_out, qkv_grad, w_qkv, w_out, doc_ids):
    d, t = lax.axis_index("dp"), lax.axis_index("tensor")
    z, yh = d // 2, d % 2
    x, yl, core = t // 4, t // 2 % 2, t % 2
    spot = (z, yh, t)
    factor = 1.0 / math.sqrt(NZ * 2 * TB)

    g_all = lax.all_gather(out_grad, "tensor", axis=0, tiled=True)
    x_all = lax.all_gather(inputs, "tensor", axis=0, tiled=True)

    attn_cols = attn_out.shape[1]
    aq = jnp.concatenate([attn_out, qkv_grad], axis=1)
    swap = lambda both: over_yh(both[:, attn_cols:])

    ids = doc_ids[None, :]
    q0s, other = tie(over_yh(qkv_grad), over_yh(ids))
    window = jnp.where(yh == 1, jnp.concatenate([other, ids]), jnp.concatenate([ids, other]))
    window = jnp.concatenate([over_z(window, 1), window])
    u1, d1, q0s, window = tie(over_z(aq, 1), over_z(aq, -1), q0s, window)

    u1s, d1s, got = tie(swap(u1), swap(d1), over_z(window, 2))
    window = jnp.concatenate([got, window])
    window = jnp.concatenate([over_z(window, 4), window])
    u2, d2, u1s, d1s, window = tie(over_z(u1, 1), over_z(d1, -1), u1s, d1s, window)

    tables = rotary_tables(in_token_order(window, z))
    wholes = unrotate([aq], [q0s], [0], spot, tables, None)
    u3, d3, u2s, d2s, *wholes = tie(over_z(u2, 1), over_z(d2, -1), swap(u2), swap(d2), *wholes)

    wholes = unrotate([u1, d1], [u1s, d1s], [-1, 1], spot, tables, wholes)
    wholes = unrotate([u2, d2], [u2s, d2s], [-2, 2], spot, tables, wholes)
    attn_part = contract_cols(g_all, w_out).astype(jnp.bfloat16)
    f, u3s, d3s, attn_part, *wholes = tie(over_z(u3, 1), swap(u3), swap(d3), attn_part, *wholes)

    fold = Fold(attn_part, z)
    fold.step()
    wholes = unrotate([u3, d3], [u3s, d3s], [-3, 3], spot, tables, wholes)
    fold.up, fold.down, fs, *wholes = tie(fold.up, fold.down, swap(f), *wholes)
    fold.step()
    q_own, q_other, a_own = unrotate([f], [fs], [4], spot, tables, wholes)
    a_other = over_yh(a_own)

    q_of = lambda c: jnp.where(c == yh, q_own, q_other)
    sent = over_core(contract_cols(q_of(1 - core), w_qkv).astype(jnp.bfloat16))
    chip = (contract_cols(q_of(core), w_qkv) + sent.astype(jnp.float32)).astype(jnp.bfloat16)
    fold.up, fold.down, chip = tie(fold.up, fold.down, chip)
    fold.step()
    toward = lambda at: lax.dynamic_slice_in_dim(chip, at % NX * 2 * TB, 2 * TB, 0)
    total = toward(x).astype(jnp.float32)
    for steps in (1, -1, 2):
        total = total + over_x(toward(x + steps + NX), steps).astype(jnp.float32)
    keep = lax.dynamic_slice_in_dim(total, yl * TB, TB, 0)
    give = lax.dynamic_slice_in_dim(total, (1 - yl) * TB, TB, 0).astype(jnp.bfloat16)
    summed = keep + over_yl(give).astype(jnp.float32)
    input_grad = (out_grad.astype(jnp.float32) + summed).astype(jnp.bfloat16)

    fold.up, x_all = tie(fold.up, x_all)
    fold.step()
    sums = fold.sums()
    keep = lax.dynamic_slice_in_dim(sums, yh * TB, TB, 0)
    send = lax.dynamic_slice_in_dim(sums, (1 - yh) * TB, TB, 0).astype(jnp.bfloat16)
    attn_grad = (keep + over_yh(send).astype(jnp.float32)).astype(jnp.bfloat16)

    a_other, _ = tie(a_other, give)
    wqkv_grad = contract_rows(q_own, q_other, x_all, yh, factor, False, 256)
    wout_grad = contract_rows(a_own, a_other, g_all, yh, factor, True, 256)
    return (input_grad, attn_grad, wqkv_grad, wout_grad)


def solution(mesh):
    return jax.shard_map(
        shards,
        mesh=mesh,
        in_specs=(
            P("tensor", "dp"),
            P("tensor", "dp"),
            P("dp", "tensor"),
            P("dp", "tensor"),
            P("dp", "tensor"),
            P("tensor", "dp"),
            P("dp"),
        ),
        out_specs=(P("tensor", "dp"), P("dp", "tensor"), P("dp", "tensor"), P("tensor", "dp")),
        check_vma=False,
    )
```

```python
import math

import jax
import jax.numpy as jnp
from jax import lax
from jax.experimental import pallas as pl
from jax.experimental.pallas import tpu as pltpu
from jax.sharding import PartitionSpec as P

HD = 128
HQ = 96
HK = 8
ROPE_BASE = 500000.0
NZ = 8
NX = 4
TB = 128
BEHIND = 4


def over_z(value, steps):
    pairs = [(z * 2 + h, (z + steps) % NZ * 2 + h) for z in range(NZ) for h in range(2)]
    return lax.ppermute(value, "dp", pairs)


def over_yh(value):
    return lax.ppermute(value, "dp", [(d, d ^ 1) for d in range(16)])


def over_x(value, steps):
    pairs = [(x * 4 + k, (x + steps) % NX * 4 + k) for x in range(NX) for k in range(4)]
    return lax.ppermute(value, "tensor", pairs)


def over_yl(value):
    return lax.ppermute(value, "tensor", [(t, t ^ 2) for t in range(16)])


def over_core(value):
    return lax.ppermute(value, "tensor", [(t, t ^ 1) for t in range(16)])


def tie(*values):
    return lax.optimization_barrier(values)


def rotary_tables(ids, window, z):
    smaller = jnp.sum((window[None, :] < ids[:, None]).astype(jnp.int32), axis=1)
    start = jnp.maximum((z - BEHIND) * 2 * TB, 0) + smaller
    positions = z * 2 * TB + jnp.arange(2 * TB, dtype=jnp.int32) - start
    lane = jnp.arange(HD, dtype=jnp.int32)
    frequency = jnp.power(jnp.float32(ROPE_BASE), -(2.0 * (lane // 2).astype(jnp.float32)) / HD)
    angles = positions.astype(jnp.float32)[:, None] * frequency[None, :]
    sign = jnp.where(lane % 2 == 0, 1.0, -1.0)
    return jnp.cos(angles), jnp.sin(angles) * sign[None, :]


def unrotate_kernel(place_ref, own_ref, other_ref, cos_ref, sin_ref, out_ref):
    even = lax.broadcasted_iota(jnp.int32, (TB, HD), 1) % 2 == 0
    swapped = place_ref[0] == 1
    for h in range(own_ref.shape[1] // HD):
        cols = slice(h * HD, (h + 1) * HD)
        rotated = place_ref[1] + h < HQ + HK
        own, other = own_ref[:, cols], other_ref[:, cols]
        for half in range(2):
            rows = slice(half * TB, (half + 1) * TB)
            values = jnp.where(swapped, *((other, own) if half == 0 else (own, other))).astype(jnp.float32)
            partner = jnp.where(even, pltpu.roll(values, HD - 1, 1), pltpu.roll(values, 1, 1))
            cosine = jnp.where(rotated, cos_ref[rows, :], 1.0)
            sine = jnp.where(rotated, sin_ref[rows, :], 0.0)
            out_ref[rows, cols] = (values * cosine + partner * sine).astype(jnp.bfloat16)


def unrotate(own, other, tables, yh, t):
    cols = own.shape[1]
    vmem = pl.BlockSpec(memory_space=pltpu.VMEM)
    return pl.pallas_call(
        unrotate_kernel,
        out_shape=jax.ShapeDtypeStruct((2 * TB, cols), jnp.bfloat16),
        in_specs=[pl.BlockSpec(memory_space=pltpu.SMEM)] + [vmem] * 4,
        out_specs=vmem,
        cost_estimate=pl.CostEstimate(flops=20 * TB * cols, bytes_accessed=8 * TB * cols, transcendentals=0),
    )(jnp.stack([yh, t * (cols // HD)]).astype(jnp.int32), own, other, *tables)


def place(groups, places, z, wholes):
    count, n_groups = len(places), len(groups)
    parts = [g[0].shape[0] // TB for g in groups]
    widths = [g[0].shape[1] for g in groups]
    where = jnp.stack([(z + p + NZ) % NZ for p in places]).astype(jnp.int32)
    operands = [v for g in groups for v in g]
    in_specs = [pl.BlockSpec(v.shape, lambda i, s: (0, 0)) for v in operands]
    aliases = {}
    if wholes is not None:
        aliases = {1 + len(operands) + k: k for k in range(n_groups)}
        operands += wholes
        in_specs += [pl.BlockSpec(memory_space=pl.ANY)] * n_groups

    def body(where_ref, *refs):
        for g in range(n_groups):
            for k in range(count):

                @pl.when(pl.program_id(0) == k)
                def _():
                    for p in range(parts[g]):
                        refs[len(operands) + g][p, 0] = refs[g * count + k][p * TB : (p + 1) * TB, :]

    return pl.pallas_call(
        body,
        out_shape=tuple(jax.ShapeDtypeStruct((p, NZ, TB, n), jnp.bfloat16) for p, n in zip(parts, widths)),
        grid_spec=pltpu.PrefetchScalarGridSpec(
            num_scalar_prefetch=1,
            grid=(count,),
            in_specs=in_specs,
            out_specs=tuple(
                pl.BlockSpec((p, 1, TB, n), lambda i, s: (0, s[i], 0, 0)) for p, n in zip(parts, widths)
            ),
        ),
        input_output_aliases=aliases,
        cost_estimate=pl.CostEstimate(flops=0, bytes_accessed=8 * count * TB * sum(widths), transcendentals=0),
    )(where, *operands)


def rows_kernel(factor, split_left, first_ref, own_ref, other_ref, both_ref, out_ref):
    first = first_ref[0]
    total = jnp.zeros(out_ref.shape, jnp.float32)
    for part, h in ((own_ref, first), (other_ref, 1 - first)):
        tokens = both_ref[:, h].reshape(NZ * TB, both_ref.shape[-1])
        half = part[0]
        left, right = (half, tokens) if split_left else (tokens, half)
        total += lax.dot_general(left, right, (((0,), (0,)), ((), ())), preferred_element_type=jnp.float32)
    out_ref[...] = total * factor


def contract_rows(own, other, both, first, factor, split_left, tile):
    tokens, a = own[0].shape[1:]
    b = both.shape[1]
    if split_left:
        m, n = a, b
        pair = [pl.BlockSpec((1, tokens, tile), lambda i, _, k=k: (k, 0, i)) for _, k in (own, other)]
        whole = pl.BlockSpec((NZ, 2, TB, b), lambda i, _: (0, 0, 0, 0))
    else:
        m, n = b, a
        pair = [pl.BlockSpec((1, tokens, a), lambda i, _, k=k: (k, 0, 0)) for _, k in (own, other)]
        whole = pl.BlockSpec((NZ, 2, TB, tile), lambda i, _: (0, 0, 0, i))
    return pl.pallas_call(
        lambda *refs: rows_kernel(factor, split_left, *refs),
        out_shape=jax.ShapeDtypeStruct((m, n), jnp.float32),
        grid_spec=pltpu.PrefetchScalarGridSpec(
            num_scalar_prefetch=1,
            grid=(m // tile,),
            in_specs=[*pair, whole],
            out_specs=pl.BlockSpec((tile, n), lambda i, _: (i, 0)),
        ),
        compiler_params=pltpu.CompilerParams(vmem_limit_bytes=40 * 2**20),
        cost_estimate=pl.CostEstimate(
            flops=4 * tokens * a * b, bytes_accessed=4 * tokens * (a + b) + 4 * a * b, transcendentals=0
        ),
    )(jnp.reshape(first, (1,)).astype(jnp.int32), own[0], other[0], both.reshape(NZ, 2, TB, b))


def contract_cols(left, right):
    return lax.dot_general(
        left, right, (((1,), (1,)), ((), ())), preferred_element_type=jnp.float32
    )


class Fold:
    def __init__(self, partial, z):
        self.partial, self.z = partial, z
        self.rows = partial.shape[0] // NZ
        self.up = self.down = None
        self.k = 4

    def mine(self, at):
        return lax.dynamic_slice_in_dim(self.partial, at % NZ * self.rows, self.rows, 0).astype(jnp.float32)

    def add(self, part, got):
        return (part if got is None else part + got.astype(jnp.float32)).astype(jnp.bfloat16)

    def step(self):
        k = self.k
        self.k -= 1
        if k < 4:
            self.up = over_z(self.add(self.mine(self.z + k), self.up), 1)
        self.down = over_z(self.add(self.mine(self.z - k + NZ), self.down), -1)

    def sums(self):
        return self.mine(self.z) + self.up.astype(jnp.float32) + self.down.astype(jnp.float32)


def shards(inputs, out_grad, attn_out, qkv_grad, w_qkv, w_out, doc_ids):
    d, t = lax.axis_index("dp"), lax.axis_index("tensor")
    z, yh = d // 2, d % 2
    x, yl, core = t // 4, t // 2 % 2, t % 2
    factor = 1.0 / math.sqrt(NZ * 2 * TB)

    g_all = lax.all_gather(out_grad, "tensor", axis=0, tiled=True)
    x_all = lax.all_gather(inputs, "tensor", axis=0, tiled=True)

    ids = doc_ids[None, :]
    q_other = over_yh(qkv_grad)
    behind = [over_z(ids, k) for k in range(1, BEHIND + 1)]
    own_ids = jnp.concatenate([ids, *behind])
    other_ids = over_yh(own_ids)
    a, _ = tie(attn_out, own_ids)
    u1, d1 = over_z(a, 1), over_z(a, -1)
    pair_ids = jnp.where(yh == 1, jnp.stack([other_ids[0], doc_ids]), jnp.stack([doc_ids, other_ids[0]]))
    window = jnp.concatenate([own_ids, other_ids]).reshape(-1)
    tables = rotary_tables(pair_ids.reshape(-1), window, z)
    pair = unrotate(qkv_grad, q_other, tables, yh, t)

    pair, u1, d1 = tie(pair, u1, d1)
    pu1, pd1, u2, d2 = tie(over_z(pair, 1), over_z(pair, -1), over_z(u1, 1), over_z(d1, -1))

    wholes = place([[pair], [attn_out]], [0], z, None)
    pu2, pd2, u3, d3, *wholes = tie(over_z(pu1, 1), over_z(pd1, -1), over_z(u2, 1), over_z(d2, -1), *wholes)

    wholes = place([[pu1, pd1], [u1, d1]], [-1, 1], z, wholes)
    attn_part = contract_cols(g_all, w_out).astype(jnp.bfloat16)
    pu3, pd3, d4, attn_part, *wholes = tie(over_z(pu2, 1), over_z(pd2, -1), over_z(d3, -1), attn_part, *wholes)

    fold = Fold(attn_part, z)
    fold.step()
    wholes = place([[pu2, pd2], [u2, d2]], [-2, 2], z, wholes)
    q_all, a_own = place([[pu3, pd3], [u3, d3]], [-3, 3], z, wholes)
    (a_own,) = place([[d4]], [4], z, [a_own])
    p4, fold.down, q_all, a_own = tie(over_z(pu3, 1), fold.down, q_all, a_own)
    (q_all,) = place([[p4]], [4], z, [q_all])
    a_own = a_own.reshape(1, NZ * TB, -1)
    a_other = over_yh(a_own)

    cols = qkv_grad.shape[1]
    q_all = q_all.reshape(2, NZ * TB, cols)
    q_of = lambda c: lax.dynamic_index_in_dim(q_all, c, 0, False)
    part = contract_cols(q_of(1 - core), w_qkv).astype(jnp.bfloat16)
    fold.down, part = tie(fold.down, part)
    sent = over_core(part)
    fold.step()
    chip = (contract_cols(q_of(core), w_qkv) + sent.astype(jnp.float32)).astype(jnp.bfloat16)
    fold.up, fold.down, _ = tie(fold.up, fold.down, chip)
    fold.step()
    toward = lambda at: lax.dynamic_slice_in_dim(chip, at % NX * 2 * TB, 2 * TB, 0)
    total = toward(x).astype(jnp.float32)
    for steps in (1, -1, 2):
        total = total + over_x(toward(x + steps + NX), steps).astype(jnp.float32)
    keep = lax.dynamic_slice_in_dim(total, yl * TB, TB, 0)
    give = lax.dynamic_slice_in_dim(total, (1 - yl) * TB, TB, 0).astype(jnp.bfloat16)
    summed = keep + over_yl(give).astype(jnp.float32)
    input_grad = (out_grad.astype(jnp.float32) + summed).astype(jnp.bfloat16)

    fold.up, x_all, a_other = tie(fold.up, x_all, a_other)
    fold.step()
    sums = fold.sums()
    keep = lax.dynamic_slice_in_dim(sums, yh * TB, TB, 0)
    send = lax.dynamic_slice_in_dim(sums, (1 - yh) * TB, TB, 0).astype(jnp.bfloat16)
    attn_grad = (keep + over_yh(send).astype(jnp.float32)).astype(jnp.bfloat16)

    a_other, _, _ = tie(a_other, give, send)
    wqkv_grad = contract_rows((q_all, 0), (q_all, 1), x_all, jnp.int32(0), factor, False, 256)
    wout_grad = contract_rows((a_own, 0), (a_other, 0), g_all, yh, factor, True, 256)
    return (input_grad, attn_grad, wqkv_grad, wout_grad)


def solution(mesh):
    return jax.shard_map(
        shards,
        mesh=mesh,
        in_specs=(
            P("tensor", "dp"),
            P("tensor", "dp"),
            P("dp", "tensor"),
            P("dp", "tensor"),
            P("dp", "tensor"),
            P("tensor", "dp"),
            P("dp"),
        ),
        out_specs=(P("tensor", "dp"), P("dp", "tensor"), P("dp", "tensor"), P("tensor", "dp")),
        check_vma=False,
    )
```

```python
import math

import jax
import jax.numpy as jnp
from jax import lax
from jax.experimental import pallas as pl
from jax.experimental.pallas import tpu as pltpu
from jax.sharding import PartitionSpec as P

HD = 128
HQ = 96
HK = 8
ROPE_BASE = 500000.0
NZ = 8
NX = 4
TB = 128
BEHIND = 4


def over_z(value, steps):
    pairs = [(z * 2 + h, (z + steps) % NZ * 2 + h) for z in range(NZ) for h in range(2)]
    return lax.ppermute(value, "dp", pairs)


def over_yh(value):
    return lax.ppermute(value, "dp", [(d, d ^ 1) for d in range(16)])


def over_x(value, steps):
    pairs = [(x * 4 + k, (x + steps) % NX * 4 + k) for x in range(NX) for k in range(4)]
    return lax.ppermute(value, "tensor", pairs)


def over_yl(value):
    return lax.ppermute(value, "tensor", [(t, t ^ 2) for t in range(16)])


def over_core(value):
    return lax.ppermute(value, "tensor", [(t, t ^ 1) for t in range(16)])


def tie(*values):
    return lax.optimization_barrier(values)


def rotary_tables(ids, window, z):
    smaller = jnp.sum((window[None, :] < ids[:, None]).astype(jnp.int32), axis=1)
    start = jnp.maximum((z - BEHIND) * 2 * TB, 0) + smaller
    positions = z * 2 * TB + jnp.arange(2 * TB, dtype=jnp.int32) - start
    lane = jnp.arange(HD, dtype=jnp.int32)
    frequency = jnp.power(jnp.float32(ROPE_BASE), -(2.0 * (lane // 2).astype(jnp.float32)) / HD)
    angles = positions.astype(jnp.float32)[:, None] * frequency[None, :]
    sign = jnp.where(lane % 2 == 0, 1.0, -1.0)
    return jnp.cos(angles), jnp.sin(angles) * sign[None, :]


def unrotate_kernel(where_ref, own_ref, other_ref, cos_ref, sin_ref, up_attn_ref, down_attn_ref, up_ref, down_ref):
    even = lax.broadcasted_iota(jnp.int32, (TB, HD), 1) % 2 == 0
    swapped = where_ref[0] == 1
    cols = own_ref.shape[1]
    for h in range(cols // HD):
        part = slice(h * HD, (h + 1) * HD)
        rotated = where_ref[1] + h < HQ + HK
        own, other = own_ref[:, part], other_ref[:, part]
        for half in range(2):
            rows = slice(half * TB, (half + 1) * TB)
            values = jnp.where(swapped, *((other, own) if half == 0 else (own, other))).astype(jnp.float32)
            partner = jnp.where(even, pltpu.roll(values, HD - 1, 1), pltpu.roll(values, 1, 1))
            cosine = jnp.where(rotated, cos_ref[rows, :], 1.0)
            sine = jnp.where(rotated, sin_ref[rows, :], 0.0)
            result = (values * cosine + partner * sine).astype(jnp.bfloat16)
            at = slice(half * cols + h * HD, half * cols + (h + 1) * HD)
            up_ref[:, at] = result
            down_ref[:, at] = result
    up_ref[:, 2 * cols :] = up_attn_ref[...]
    down_ref[:, 2 * cols :] = down_attn_ref[...]


def unrotate(own, other, tables, up_attn, down_attn, yh, t):
    cols = own.shape[1]
    vmem = pl.BlockSpec(memory_space=pltpu.VMEM)
    shape = jax.ShapeDtypeStruct((TB, 2 * cols + up_attn.shape[1]), jnp.bfloat16)
    return pl.pallas_call(
        unrotate_kernel,
        out_shape=(shape, shape),
        in_specs=[pl.BlockSpec(memory_space=pltpu.SMEM)] + [vmem] * 6,
        out_specs=(vmem, vmem),
        cost_estimate=pl.CostEstimate(flops=20 * TB * cols, bytes_accessed=16 * TB * cols, transcendentals=0),
    )(jnp.stack([yh, t * (cols // HD)]).astype(jnp.int32), own, other, *tables, up_attn, down_attn)


def place_first(block, count):
    def body(block_ref, out_ref):
        out_ref[0] = block_ref[...]

    n = block.shape[1]
    return pl.pallas_call(
        body,
        out_shape=jax.ShapeDtypeStruct((count, TB, n), jnp.bfloat16),
        grid=(1,),
        in_specs=[pl.BlockSpec((TB, n), lambda i: (0, 0))],
        out_specs=pl.BlockSpec((1, TB, n), lambda i: (0, 0, 0)),
    )(block)


def absorb(blocks, q_places, a_places, z, core, weights, wholes):
    count, with_attn = len(blocks), bool(a_places)
    width, cols = weights.shape
    attn_cols = blocks[0].shape[1] - 2 * cols
    at = lambda p: (z + p + NZ) % NZ
    where = jnp.stack([*map(at, q_places), core]).astype(jnp.int32)
    q_spec = pl.BlockSpec((2, 1, TB, cols), lambda i, s: (0, s[i], 0, 0))
    share = pl.BlockSpec((1, TB, width), lambda i, s: (s[i], 0, 0))
    out_specs = [q_spec, share, share]
    out_shape = [jax.ShapeDtypeStruct((2, NZ, TB, cols), jnp.bfloat16)]
    out_shape += [jax.ShapeDtypeStruct((NZ, TB, width), jnp.bfloat16)] * 2
    if with_attn:
        first, total = a_places
        out_specs.append(pl.BlockSpec((1, TB, attn_cols), lambda i, s: (jnp.minimum(first + i, total - 1), 0, 0)))
        out_shape.append(jax.ShapeDtypeStruct((total, TB, attn_cols), jnp.bfloat16))
    operands = [*blocks, weights]
    in_specs = [pl.BlockSpec(v.shape, lambda i, s: (0, 0)) for v in operands]
    aliases = {}
    for k, whole in enumerate(wholes):
        if whole is not None:
            aliases[1 + len(operands)] = k
            operands.append(whole)
            in_specs.append(pl.BlockSpec(memory_space=pltpu.HBM))
    n_out = len(out_specs)

    def body(where_ref, *refs):
        weights_ref = refs[count]
        outs = refs[-n_out:]
        first = where_ref[count] == 0
        for k in range(count):

            @pl.when(pl.program_id(0) == k)
            def _():
                halves = [refs[k][:, :cols], refs[k][:, cols : 2 * cols]]
                outs[0][0, 0], outs[0][1, 0] = halves
                if with_attn:
                    outs[3][0] = refs[k][:, 2 * cols :]
                product = lax.dot_general(
                    jnp.concatenate(halves),
                    weights_ref[...],
                    (((1,), (1,)), ((), ())),
                    preferred_element_type=jnp.float32,
                ).astype(jnp.bfloat16)
                outs[1][0] = jnp.where(first, product[:TB], product[TB:])
                outs[2][0] = jnp.where(first, product[TB:], product[:TB])

    return pl.pallas_call(
        body,
        out_shape=tuple(out_shape),
        grid_spec=pltpu.PrefetchScalarGridSpec(
            num_scalar_prefetch=1, grid=(count,), in_specs=in_specs, out_specs=tuple(out_specs)
        ),
        input_output_aliases=aliases,
        compiler_params=pltpu.CompilerParams(vmem_limit_bytes=60 * 2**20),
        cost_estimate=pl.CostEstimate(
            flops=4 * count * TB * cols * width,
            bytes_accessed=2 * width * cols + 4 * count * TB * (2 * cols + attn_cols + width),
            transcendentals=0,
        ),
    )(where, *operands)


def contract_rows(left, right, factor, tile):
    m, n = left.shape[1], right.shape[2]

    def body(left_ref, right_ref, out_ref):
        total = jnp.zeros(out_ref.shape, jnp.float32)
        for h in range(2):
            tokens = left_ref[:, h].reshape(NZ * TB, tile)
            total += lax.dot_general(
                tokens, right_ref[h], (((0,), (0,)), ((), ())), preferred_element_type=jnp.float32
            )
        out_ref[...] = total * factor

    return pl.pallas_call(
        body,
        out_shape=jax.ShapeDtypeStruct((m, n), jnp.float32),
        grid=(m // tile,),
        in_specs=[
            pl.BlockSpec((NZ, 2, TB, tile), lambda i: (0, 0, 0, i)),
            pl.BlockSpec(right.shape, lambda i: (0, 0, 0)),
        ],
        out_specs=pl.BlockSpec((tile, n), lambda i: (i, 0)),
        compiler_params=pltpu.CompilerParams(vmem_limit_bytes=60 * 2**20),
        cost_estimate=pl.CostEstimate(
            flops=4 * NZ * TB * m * n, bytes_accessed=4 * NZ * TB * (m + n) + 4 * m * n, transcendentals=0
        ),
    )(left.reshape(NZ, 2, TB, m), right)


def ring_rows(chunks, both, order, yh, factor, tile):
    m, n = chunks[0][0].shape[2], both.shape[1]
    operands = [v for chunk in chunks for v in chunk]

    def body(where_ref, *refs):
        both_ref, out_ref = refs[-2:]
        total = jnp.zeros(out_ref.shape, jnp.float32)
        for side in range(2):
            h = where_ref[NZ] if side == 0 else 1 - where_ref[NZ]
            first = 0
            for c in range(len(chunks)):
                part = refs[2 * c + side]
                k = part.shape[0]
                tokens = jnp.concatenate([both_ref[where_ref[first + j], h] for j in range(k)])
                left = part[...].reshape(k * TB, tile)
                total += lax.dot_general(left, tokens, (((0,), (0,)), ((), ())), preferred_element_type=jnp.float32)
                first += k
        out_ref[...] = total * factor

    return pl.pallas_call(
        body,
        out_shape=jax.ShapeDtypeStruct((m, n), jnp.float32),
        grid_spec=pltpu.PrefetchScalarGridSpec(
            num_scalar_prefetch=1,
            grid=(m // tile,),
            in_specs=[pl.BlockSpec((v.shape[0], TB, tile), lambda i, s: (0, 0, i)) for v in operands]
            + [pl.BlockSpec((NZ, 2, TB, n), lambda i, s: (0, 0, 0, 0))],
            out_specs=pl.BlockSpec((tile, n), lambda i, s: (i, 0)),
        ),
        compiler_params=pltpu.CompilerParams(vmem_limit_bytes=60 * 2**20),
        cost_estimate=pl.CostEstimate(
            flops=4 * NZ * TB * m * n, bytes_accessed=4 * NZ * TB * (m + n) + 4 * m * n, transcendentals=0
        ),
    )(jnp.stack([*order, yh]).astype(jnp.int32), *operands, both.reshape(NZ, 2, TB, n))


def contract_cols(left, right):
    return lax.dot_general(
        left, right, (((1,), (1,)), ((), ())), preferred_element_type=jnp.float32
    )


class Fold:
    def __init__(self, partial, z):
        self.partial, self.z = partial, z
        self.rows = partial.shape[0] // NZ
        self.up = self.down = None
        self.k = 4

    def mine(self, at):
        return lax.dynamic_slice_in_dim(self.partial, at % NZ * self.rows, self.rows, 0).astype(jnp.float32)

    def add(self, part, got):
        return (part if got is None else part + got.astype(jnp.float32)).astype(jnp.bfloat16)

    def step(self):
        k = self.k
        self.k -= 1
        if k < 4:
            self.up = over_z(self.add(self.mine(self.z + k), self.up), 1)
        self.down = over_z(self.add(self.mine(self.z - k + NZ), self.down), -1)

    def sums(self):
        return self.mine(self.z) + self.up.astype(jnp.float32) + self.down.astype(jnp.float32)


def shards(inputs, out_grad, attn_out, qkv_grad, w_qkv, w_out, doc_ids):
    d, t = lax.axis_index("dp"), lax.axis_index("tensor")
    z, yh = d // 2, d % 2
    x, yl, core = t // 4, t // 2 % 2, t % 2
    factor = 1.0 / math.sqrt(NZ * 2 * TB)

    g_all = lax.all_gather(out_grad, "tensor", axis=0, tiled=True)
    x_all = lax.all_gather(inputs, "tensor", axis=0, tiled=True)

    ids = doc_ids[None, :]
    other_ids = over_yh(ids)
    q_other = over_yh(qkv_grad)
    pair_ids = jnp.where(yh == 1, jnp.concatenate([other_ids, ids]), jnp.concatenate([ids, other_ids]))
    near = [over_z(pair_ids, 1), over_z(pair_ids, 2)]
    attn, _ = tie(attn_out, pair_ids)
    up_attn, down_attn = over_z(attn, 1), over_z(attn, -1)
    far = over_z(jnp.concatenate(near), 2)
    window = jnp.concatenate([pair_ids, *near, far]).reshape(-1)
    tables = rotary_tables(pair_ids.reshape(-1), window, z)

    up0, down0 = unrotate(qkv_grad, q_other, tables, up_attn, down_attn, yh, t)
    up1, down1 = tie(over_z(up0, 1), over_z(down0, -1))

    attn1 = place_first(attn_out, 5)
    *shares, attn1 = absorb([up0, down0], [0, 0], (1, 5), z, core, w_qkv, [None, None, None, attn1])
    *shares, attn1 = absorb([up1, down1], [-1, 1], (3, 5), z, core, w_qkv, [*shares, attn1])
    up2, down2, attn1, *shares = tie(over_z(up1, 1), over_z(down1, -1), attn1, *shares)

    *shares, attn2 = absorb([up2, down2], [-2, 2], (0, 3), z, core, w_qkv, [*shares, None])
    attn_part = contract_cols(g_all, w_out).astype(jnp.bfloat16)
    up3, down3, attn_part, attn2, *shares = tie(over_z(up2, 1), over_z(down2, -1), attn_part, attn2, *shares)

    attn1_other = over_yh(attn1)
    fold = Fold(attn_part, z)
    fold.step()
    last = over_z(up3[:, : 2 * qkv_grad.shape[1]], 1)
    *shares, attn2 = absorb([up3, down3], [-3, 3], (2, 3), z, core, w_qkv, [*shares, attn2])
    last, fold.down, *shares = tie(last, fold.down, *shares)
    q_all, kept, given = absorb([last], [4], None, z, core, w_qkv, shares)

    q_all = q_all.reshape(2, NZ * TB, -1)
    sent = over_core(given)
    fold.step()
    chip = (kept.astype(jnp.float32) + sent.astype(jnp.float32)).astype(jnp.bfloat16).reshape(NZ * TB, -1)
    fold.up, fold.down, x_all, attn1_other, attn2, _ = tie(fold.up, fold.down, x_all, attn1_other, attn2, chip)
    attn2_other = over_yh(attn2)
    fold.step()
    toward = lambda at: lax.dynamic_slice_in_dim(chip, at % NX * 2 * TB, 2 * TB, 0)
    total = toward(x).astype(jnp.float32)
    for steps in (1, -1, 2):
        total = total + over_x(toward(x + steps + NX), steps).astype(jnp.float32)
    keep = lax.dynamic_slice_in_dim(total, yl * TB, TB, 0)
    give = lax.dynamic_slice_in_dim(total, (1 - yl) * TB, TB, 0).astype(jnp.bfloat16)
    summed = keep + over_yl(give).astype(jnp.float32)
    input_grad = (out_grad.astype(jnp.float32) + summed).astype(jnp.bfloat16)

    fold.step()
    sums = fold.sums()
    keep = lax.dynamic_slice_in_dim(sums, yh * TB, TB, 0)
    send = lax.dynamic_slice_in_dim(sums, (1 - yh) * TB, TB, 0).astype(jnp.bfloat16)
    attn_grad = (keep + over_yh(send).astype(jnp.float32)).astype(jnp.bfloat16)

    attn2_other, _, _ = tie(attn2_other, give, send)
    wqkv_grad = contract_rows(x_all, q_all, factor, 256)
    order = [(z + p + NZ) % NZ for p in (0, -1, 1, -2, 2, -3, 3, 4)]
    wout_grad = ring_rows([(attn1, attn1_other), (attn2, attn2_other)], g_all, order, yh, factor, 256)
    return (input_grad, attn_grad, wqkv_grad, wout_grad)


def solution(mesh):
    return jax.shard_map(
        shards,
        mesh=mesh,
        in_specs=(
            P("tensor", "dp"),
            P("tensor", "dp"),
            P("dp", "tensor"),
            P("dp", "tensor"),
            P("dp", "tensor"),
            P("tensor", "dp"),
            P("dp"),
        ),
        out_specs=(P("tensor", "dp"), P("dp", "tensor"), P("dp", "tensor"), P("tensor", "dp")),
        check_vma=False,
    )
```

```python
import math

import jax
import jax.numpy as jnp
from jax import lax
from jax.experimental import pallas as pl
from jax.experimental.pallas import tpu as pltpu
from jax.sharding import PartitionSpec as P

HD = 128
HQ = 96
HK = 8
ROPE_BASE = 500000.0
NZ = 8
NX = 4
TB = 128
BEHIND = 4


def over_z(value, steps):
    pairs = [(z * 2 + h, (z + steps) % NZ * 2 + h) for z in range(NZ) for h in range(2)]
    return lax.ppermute(value, "dp", pairs)


def over_yh(value):
    return lax.ppermute(value, "dp", [(d, d ^ 1) for d in range(16)])


def over_x(value, steps):
    pairs = [(x * 4 + k, (x + steps) % NX * 4 + k) for x in range(NX) for k in range(4)]
    return lax.ppermute(value, "tensor", pairs)


def over_yl(value):
    return lax.ppermute(value, "tensor", [(t, t ^ 2) for t in range(16)])


def over_core(value):
    return lax.ppermute(value, "tensor", [(t, t ^ 1) for t in range(16)])


def tie(*values):
    return lax.optimization_barrier(values)


def rotary_tables(ids, window, z):
    smaller = jnp.sum((window[None, :] < ids[:, None]).astype(jnp.int32), axis=1)
    start = jnp.maximum((z - BEHIND) * 2 * TB, 0) + smaller
    positions = z * 2 * TB + jnp.arange(2 * TB, dtype=jnp.int32) - start
    lane = jnp.arange(HD, dtype=jnp.int32)
    frequency = jnp.power(jnp.float32(ROPE_BASE), -(2.0 * (lane // 2).astype(jnp.float32)) / HD)
    angles = positions.astype(jnp.float32)[:, None] * frequency[None, :]
    sign = jnp.where(lane % 2 == 0, 1.0, -1.0)
    return jnp.cos(angles), jnp.sin(angles) * sign[None, :]


def unrotate_kernel(where_ref, own_ref, other_ref, cos_ref, sin_ref, up_attn_ref, down_attn_ref, up_ref, down_ref):
    even = lax.broadcasted_iota(jnp.int32, (TB, HD), 1) % 2 == 0
    swapped = where_ref[0] == 1
    cols = own_ref.shape[1]
    for h in range(cols // HD):
        part = slice(h * HD, (h + 1) * HD)
        rotated = where_ref[1] + h < HQ + HK
        own, other = own_ref[:, part], other_ref[:, part]
        for half in range(2):
            rows = slice(half * TB, (half + 1) * TB)
            values = jnp.where(swapped, *((other, own) if half == 0 else (own, other))).astype(jnp.float32)
            partner = jnp.where(even, pltpu.roll(values, HD - 1, 1), pltpu.roll(values, 1, 1))
            cosine = jnp.where(rotated, cos_ref[rows, :], 1.0)
            sine = jnp.where(rotated, sin_ref[rows, :], 0.0)
            result = (values * cosine + partner * sine).astype(jnp.bfloat16)
            at = slice(half * cols + h * HD, half * cols + (h + 1) * HD)
            up_ref[:, at] = result
            down_ref[:, at] = result
    up_ref[:, 2 * cols :] = up_attn_ref[...]
    down_ref[:, 2 * cols :] = down_attn_ref[...]


def unrotate(own, other, tables, up_attn, down_attn, yh, t):
    cols = own.shape[1]
    vmem = pl.BlockSpec(memory_space=pltpu.VMEM)
    shape = jax.ShapeDtypeStruct((TB, 2 * cols + up_attn.shape[1]), jnp.bfloat16)
    return pl.pallas_call(
        unrotate_kernel,
        out_shape=(shape, shape),
        in_specs=[pl.BlockSpec(memory_space=pltpu.SMEM)] + [vmem] * 6,
        out_specs=(vmem, vmem),
        cost_estimate=pl.CostEstimate(flops=20 * TB * cols, bytes_accessed=16 * TB * cols, transcendentals=0),
    )(jnp.stack([yh, t * (cols // HD)]).astype(jnp.int32), own, other, *tables, up_attn, down_attn)


def place_first(block, count):
    def body(block_ref, out_ref):
        out_ref[0] = block_ref[...]

    n = block.shape[1]
    return pl.pallas_call(
        body,
        out_shape=jax.ShapeDtypeStruct((count, TB, n), jnp.bfloat16),
        grid=(1,),
        in_specs=[pl.BlockSpec((TB, n), lambda i: (0, 0))],
        out_specs=pl.BlockSpec((1, TB, n), lambda i: (0, 0, 0)),
    )(block)


def absorb(blocks, q_places, a_places, z, core, weights, wholes):
    count, with_attn = len(blocks), bool(a_places)
    cols, width = weights.shape
    attn_cols = blocks[0].shape[1] - 2 * cols
    at = lambda p: (z + p + NZ) % NZ
    where = jnp.stack([*map(at, q_places), core]).astype(jnp.int32)
    q_spec = pl.BlockSpec((2, 1, TB, cols), lambda i, s: (0, s[i], 0, 0))
    share = pl.BlockSpec((1, TB, width), lambda i, s: (s[i], 0, 0))
    out_specs = [q_spec, share, share]
    out_shape = [jax.ShapeDtypeStruct((2, NZ, TB, cols), jnp.bfloat16)]
    out_shape += [jax.ShapeDtypeStruct((NZ, TB, width), jnp.bfloat16)] * 2
    if with_attn:
        first, total = a_places
        out_specs.append(pl.BlockSpec((1, TB, attn_cols), lambda i, s: (jnp.minimum(first + i, total - 1), 0, 0)))
        out_shape.append(jax.ShapeDtypeStruct((total, TB, attn_cols), jnp.bfloat16))
    operands = [*blocks, weights]
    in_specs = [pl.BlockSpec(v.shape, lambda i, s: (0, 0)) for v in operands]
    aliases = {}
    for k, whole in enumerate(wholes):
        if whole is not None:
            aliases[1 + len(operands)] = k
            operands.append(whole)
            in_specs.append(pl.BlockSpec(memory_space=pltpu.HBM))
    n_out = len(out_specs)

    def body(where_ref, *refs):
        weights_ref = refs[count]
        outs = refs[-n_out:]
        first = where_ref[count] == 0
        for k in range(count):

            @pl.when(pl.program_id(0) == k)
            def _():
                halves = [refs[k][:, :cols], refs[k][:, cols : 2 * cols]]
                outs[0][0, 0], outs[0][1, 0] = halves
                if with_attn:
                    outs[3][0] = refs[k][:, 2 * cols :]
                product = jnp.dot(
                    jnp.concatenate(halves), weights_ref[...], preferred_element_type=jnp.float32
                ).astype(jnp.bfloat16)
                outs[1][0] = jnp.where(first, product[:TB], product[TB:])
                outs[2][0] = jnp.where(first, product[TB:], product[:TB])

    return pl.pallas_call(
        body,
        out_shape=tuple(out_shape),
        grid_spec=pltpu.PrefetchScalarGridSpec(
            num_scalar_prefetch=1, grid=(count,), in_specs=in_specs, out_specs=tuple(out_specs)
        ),
        input_output_aliases=aliases,
        compiler_params=pltpu.CompilerParams(vmem_limit_bytes=60 * 2**20),
        cost_estimate=pl.CostEstimate(
            flops=4 * count * TB * cols * width,
            bytes_accessed=2 * width * cols + 4 * count * TB * (2 * cols + attn_cols + width),
            transcendentals=0,
        ),
    )(where, *operands)


def chip_parts(kept, sent, targets):
    n = kept.shape[2]
    count = len(targets)
    pair = pl.BlockSpec((2, TB, n), lambda i, s: (s[i], 0, 0))

    def body(where_ref, kept_ref, sent_ref, *outs):
        total = (kept_ref[...].astype(jnp.float32) + sent_ref[...].astype(jnp.float32)).astype(jnp.bfloat16)
        for k in range(count):

            @pl.when(pl.program_id(0) == k)
            def _():
                outs[k][...] = total.reshape(2 * TB, n)

    return pl.pallas_call(
        body,
        out_shape=(jax.ShapeDtypeStruct((2 * TB, n), jnp.bfloat16),) * count,
        grid_spec=pltpu.PrefetchScalarGridSpec(
            num_scalar_prefetch=1,
            grid=(count,),
            in_specs=[pair, pair],
            out_specs=(pl.BlockSpec((2 * TB, n), lambda i, s: (0, 0)),) * count,
        ),
        cost_estimate=pl.CostEstimate(flops=NZ * TB * n, bytes_accessed=6 * NZ * TB * n, transcendentals=0),
    )(jnp.stack(targets).astype(jnp.int32), kept, sent)


def contract_rows(left, right, factor, tile):
    m, n = left.shape[1], right.shape[2]

    def body(left_ref, right_ref, out_ref):
        total = jnp.zeros(out_ref.shape, jnp.float32)
        for h in range(2):
            tokens = left_ref[:, h].reshape(NZ * TB, tile)
            total += lax.dot_general(
                tokens, right_ref[h], (((0,), (0,)), ((), ())), preferred_element_type=jnp.float32
            )
        out_ref[...] = total * factor

    return pl.pallas_call(
        body,
        out_shape=jax.ShapeDtypeStruct((m, n), jnp.float32),
        grid=(m // tile,),
        in_specs=[
            pl.BlockSpec((NZ, 2, TB, tile), lambda i: (0, 0, 0, i)),
            pl.BlockSpec(right.shape, lambda i: (0, 0, 0)),
        ],
        out_specs=pl.BlockSpec((tile, n), lambda i: (i, 0)),
        compiler_params=pltpu.CompilerParams(vmem_limit_bytes=40 * 2**20),
        cost_estimate=pl.CostEstimate(
            flops=4 * NZ * TB * m * n, bytes_accessed=4 * NZ * TB * (m + n) + 4 * m * n, transcendentals=0
        ),
    )(left.reshape(NZ, 2, TB, m), right)


def ring_rows(chunks, both, order, yh, factor, tile):
    m, n = chunks[0][0].shape[2], both.shape[1]
    operands = [v for chunk in chunks for v in chunk]

    def body(where_ref, *refs):
        both_ref, out_ref = refs[-2:]
        total = jnp.zeros(out_ref.shape, jnp.float32)
        for side in range(2):
            h = where_ref[NZ] if side == 0 else 1 - where_ref[NZ]
            first = 0
            for c in range(len(chunks)):
                part = refs[2 * c + side]
                k = part.shape[0]
                tokens = jnp.concatenate([both_ref[where_ref[first + j], h] for j in range(k)])
                left = part[...].reshape(k * TB, tile)
                total += lax.dot_general(left, tokens, (((0,), (0,)), ((), ())), preferred_element_type=jnp.float32)
                first += k
        out_ref[...] = total * factor

    return pl.pallas_call(
        body,
        out_shape=jax.ShapeDtypeStruct((m, n), jnp.float32),
        grid_spec=pltpu.PrefetchScalarGridSpec(
            num_scalar_prefetch=1,
            grid=(m // tile,),
            in_specs=[pl.BlockSpec((v.shape[0], TB, tile), lambda i, s: (0, 0, i)) for v in operands]
            + [pl.BlockSpec((NZ, 2, TB, n), lambda i, s: (0, 0, 0, 0))],
            out_specs=pl.BlockSpec((tile, n), lambda i, s: (i, 0)),
        ),
        compiler_params=pltpu.CompilerParams(vmem_limit_bytes=40 * 2**20),
        cost_estimate=pl.CostEstimate(
            flops=4 * NZ * TB * m * n, bytes_accessed=4 * NZ * TB * (m + n) + 4 * m * n, transcendentals=0
        ),
    )(jnp.stack([*order, yh]).astype(jnp.int32), *operands, both.reshape(NZ, 2, TB, n))


def contract_cols(left, right):
    return lax.dot_general(
        left, right, (((1,), (1,)), ((), ())), preferred_element_type=jnp.float32
    )


class Fold:
    def __init__(self, partial, z):
        self.partial, self.z = partial, z
        self.rows = partial.shape[0] // NZ
        self.up = self.down = None
        self.k = 4

    def mine(self, at):
        return lax.dynamic_slice_in_dim(self.partial, at % NZ * self.rows, self.rows, 0).astype(jnp.float32)

    def add(self, part, got):
        return (part if got is None else part + got.astype(jnp.float32)).astype(jnp.bfloat16)

    def step(self):
        k = self.k
        self.k -= 1
        if k < 4:
            self.up = over_z(self.add(self.mine(self.z + k), self.up), 1)
        self.down = over_z(self.add(self.mine(self.z - k + NZ), self.down), -1)

    def sums(self):
        return self.mine(self.z) + self.up.astype(jnp.float32) + self.down.astype(jnp.float32)


def shards(inputs, out_grad, attn_out, qkv_grad, w_qkv, w_out, doc_ids):
    d, t = lax.axis_index("dp"), lax.axis_index("tensor")
    z, yh = d // 2, d % 2
    x, yl, core = t // 4, t // 2 % 2, t % 2
    factor = 1.0 / math.sqrt(NZ * 2 * TB)

    g_all = lax.all_gather(out_grad, "tensor", axis=0, tiled=True)
    x_all = lax.all_gather(inputs, "tensor", axis=0, tiled=True)

    ids = doc_ids[None, :]
    other_ids = over_yh(ids)
    q_other = over_yh(qkv_grad)
    pair_ids = jnp.where(yh == 1, jnp.concatenate([other_ids, ids]), jnp.concatenate([ids, other_ids]))
    near = [over_z(pair_ids, 1), over_z(pair_ids, 2)]
    attn, _ = tie(attn_out, pair_ids)
    up_attn, down_attn = over_z(attn, 1), over_z(attn, -1)
    far = over_z(jnp.concatenate(near), 2)
    window = jnp.concatenate([pair_ids, *near, far]).reshape(-1)
    tables = rotary_tables(pair_ids.reshape(-1), window, z)

    up0, down0 = unrotate(qkv_grad, q_other, tables, up_attn, down_attn, yh, t)
    up0, down0, w_t = tie(up0, down0, w_qkv.T)
    up1, down1 = tie(over_z(up0, 1), over_z(down0, -1))

    attn1 = place_first(attn_out, 3)
    *shares, attn1 = absorb([up0, down0], [0, 0], (1, 3), z, core, w_t, [None, None, None, attn1])
    *shares, attn2 = absorb([up1, down1], [-1, 1], (0, 2), z, core, w_t, [*shares, None])
    up2, down2, attn1, attn2, *shares = tie(over_z(up1, 1), over_z(down1, -1), attn1, attn2, *shares)

    *shares, attn3 = absorb([up2, down2], [-2, 2], (0, 3), z, core, w_t, [*shares, None])
    attn_part = contract_cols(g_all, w_out).astype(jnp.bfloat16)
    up3, down3, attn1_other, attn_part, attn2, attn3, *shares = tie(
        over_z(up2, 1), over_z(down2, -1), over_yh(attn1), attn_part, attn2, attn3, *shares
    )

    fold = Fold(attn_part, z)
    fold.step()
    last = over_z(up3[:, : 2 * qkv_grad.shape[1]], 1)
    *shares, attn3 = absorb([up3, down3], [-3, 3], (2, 3), z, core, w_t, [*shares, attn3])
    last, fold.down, attn2_other, *shares = tie(last, fold.down, over_yh(attn2), *shares)
    q_all, kept, given = absorb([last], [4], None, z, core, w_t, shares)

    q_all = q_all.reshape(2, NZ * TB, -1)
    sent = over_core(given)
    attn3_other = over_yh(attn3)
    fold.step()
    steps = (1, -1, 2)
    mine, *away = chip_parts(kept, sent, [(x + k + NX) % NX for k in (0, *steps)])
    fold.up, fold.down, x_all, attn3_other, _ = tie(fold.up, fold.down, x_all, attn3_other, mine)
    fold.step()
    total = mine.astype(jnp.float32)
    for k, part in zip(steps, away):
        total = total + over_x(part, k).astype(jnp.float32)
    keep = lax.dynamic_slice_in_dim(total, yl * TB, TB, 0)
    give = lax.dynamic_slice_in_dim(total, (1 - yl) * TB, TB, 0).astype(jnp.bfloat16)
    summed = keep + over_yl(give).astype(jnp.float32)
    input_grad = (out_grad.astype(jnp.float32) + summed).astype(jnp.bfloat16)

    fold.step()
    sums = fold.sums()
    keep = lax.dynamic_slice_in_dim(sums, yh * TB, TB, 0)
    send = lax.dynamic_slice_in_dim(sums, (1 - yh) * TB, TB, 0).astype(jnp.bfloat16)
    attn_grad = (keep + over_yh(send).astype(jnp.float32)).astype(jnp.bfloat16)

    attn3_other, _, _ = tie(attn3_other, give, send)
    wqkv_grad = contract_rows(x_all, q_all, factor, 256)
    order = [(z + p + NZ) % NZ for p in (0, -1, 1, -2, 2, -3, 3, 4)]
    wout_grad = ring_rows([(attn1, attn1_other), (attn2, attn2_other), (attn3, attn3_other)], g_all, order, yh, factor, 256)
    return (input_grad, attn_grad, wqkv_grad, wout_grad)


def solution(mesh):
    return jax.shard_map(
        shards,
        mesh=mesh,
        in_specs=(
            P("tensor", "dp"),
            P("tensor", "dp"),
            P("dp", "tensor"),
            P("dp", "tensor"),
            P("dp", "tensor"),
            P("tensor", "dp"),
            P("dp"),
        ),
        out_specs=(P("tensor", "dp"), P("dp", "tensor"), P("dp", "tensor"), P("tensor", "dp")),
        check_vma=False,
    )
```

```python
import math

import jax
import jax.numpy as jnp
from jax import lax
from jax.experimental import pallas as pl
from jax.experimental.pallas import tpu as pltpu
from jax.sharding import PartitionSpec as P

HD = 128
HQ = 96
HK = 8
ROPE_BASE = 500000.0
NZ = 8
NX = 4
TB = 128
BEHIND = 4


def over_z(value, steps):
    pairs = [(z * 2 + h, (z + steps) % NZ * 2 + h) for z in range(NZ) for h in range(2)]
    return lax.ppermute(value, "dp", pairs)


def over_yh(value):
    return lax.ppermute(value, "dp", [(d, d ^ 1) for d in range(16)])


def over_x(value, steps):
    pairs = [(x * 4 + k, (x + steps) % NX * 4 + k) for x in range(NX) for k in range(4)]
    return lax.ppermute(value, "tensor", pairs)


def over_yl(value):
    return lax.ppermute(value, "tensor", [(t, t ^ 2) for t in range(16)])


def over_core(value):
    return lax.ppermute(value, "tensor", [(t, t ^ 1) for t in range(16)])


def tie(*values):
    return lax.optimization_barrier(values)


def rotary_tables(ids, window, z):
    smaller = jnp.sum((window[None, :] < ids[:, None]).astype(jnp.int32), axis=1)
    start = jnp.maximum((z - BEHIND) * 2 * TB, 0) + smaller
    positions = z * 2 * TB + jnp.arange(2 * TB, dtype=jnp.int32) - start
    lane = jnp.arange(HD, dtype=jnp.int32)
    frequency = jnp.power(jnp.float32(ROPE_BASE), -(2.0 * (lane // 2).astype(jnp.float32)) / HD)
    angles = positions.astype(jnp.float32)[:, None] * frequency[None, :]
    sign = jnp.where(lane % 2 == 0, 1.0, -1.0)
    return jnp.cos(angles), jnp.sin(angles) * sign[None, :]


def unrotate_kernel(where_ref, own_ref, other_ref, cos_ref, sin_ref, up_attn_ref, down_attn_ref, up_ref, down_ref):
    even = lax.broadcasted_iota(jnp.int32, (TB, HD), 1) % 2 == 0
    swapped = where_ref[0] == 1
    cols = own_ref.shape[1]
    for h in range(cols // HD):
        part = slice(h * HD, (h + 1) * HD)
        rotated = where_ref[1] + h < HQ + HK
        own, other = own_ref[:, part], other_ref[:, part]
        for half in range(2):
            rows = slice(half * TB, (half + 1) * TB)
            values = jnp.where(swapped, *((other, own) if half == 0 else (own, other))).astype(jnp.float32)
            partner = jnp.where(even, pltpu.roll(values, HD - 1, 1), pltpu.roll(values, 1, 1))
            cosine = jnp.where(rotated, cos_ref[rows, :], 1.0)
            sine = jnp.where(rotated, sin_ref[rows, :], 0.0)
            result = (values * cosine + partner * sine).astype(jnp.bfloat16)
            at = slice(half * cols + h * HD, half * cols + (h + 1) * HD)
            up_ref[:, at] = result
            down_ref[:, at] = result
    up_ref[:, 2 * cols :] = up_attn_ref[...]
    down_ref[:, 2 * cols :] = down_attn_ref[...]


def unrotate(own, other, tables, up_attn, down_attn, yh, t):
    cols = own.shape[1]
    vmem = pl.BlockSpec(memory_space=pltpu.VMEM)
    shape = jax.ShapeDtypeStruct((TB, 2 * cols + up_attn.shape[1]), jnp.bfloat16)
    return pl.pallas_call(
        unrotate_kernel,
        out_shape=(shape, shape),
        in_specs=[pl.BlockSpec(memory_space=pltpu.SMEM)] + [vmem] * 6,
        out_specs=(vmem, vmem),
        cost_estimate=pl.CostEstimate(flops=20 * TB * cols, bytes_accessed=16 * TB * cols, transcendentals=0),
    )(jnp.stack([yh, t * (cols // HD)]).astype(jnp.int32), own, other, *tables, up_attn, down_attn)


def place_first(block, z):
    def body(z_ref, block_ref, out_ref):
        out_ref[0] = block_ref[...]

    n = block.shape[1]
    return pl.pallas_call(
        body,
        out_shape=jax.ShapeDtypeStruct((NZ, TB, n), jnp.bfloat16),
        grid_spec=pltpu.PrefetchScalarGridSpec(
            num_scalar_prefetch=1,
            grid=(1,),
            in_specs=[pl.BlockSpec((TB, n), lambda i, s: (0, 0))],
            out_specs=pl.BlockSpec((1, TB, n), lambda i, s: (s[0], 0, 0)),
        ),
    )(jnp.reshape(z, (1,)).astype(jnp.int32), block)


def absorb(blocks, q_places, a_places, z, core, weights, wholes):
    count, with_attn = len(blocks), bool(a_places)
    width, cols = weights.shape
    attn_cols = blocks[0].shape[1] - 2 * cols
    at = lambda p: (z + p + NZ) % NZ
    where = jnp.stack([*map(at, q_places), core, *map(at, a_places or ())]).astype(jnp.int32)
    q_spec = pl.BlockSpec((2, 1, TB, cols), lambda i, s: (0, s[i], 0, 0))
    share = pl.BlockSpec((1, TB, width), lambda i, s: (s[i], 0, 0))
    out_specs = [q_spec, share, share]
    out_shape = [jax.ShapeDtypeStruct((2, NZ, TB, cols), jnp.bfloat16)]
    out_shape += [jax.ShapeDtypeStruct((NZ, TB, width), jnp.bfloat16)] * 2
    if with_attn:
        out_specs.append(pl.BlockSpec((1, TB, attn_cols), lambda i, s: (s[count + 1 + i], 0, 0)))
        out_shape.append(jax.ShapeDtypeStruct((NZ, TB, attn_cols), jnp.bfloat16))
    operands = [*blocks, weights]
    in_specs = [pl.BlockSpec(v.shape, lambda i, s: (0, 0)) for v in operands]
    aliases = {}
    for k, whole in enumerate(wholes):
        if whole is not None:
            aliases[1 + len(operands)] = k
            operands.append(whole)
            in_specs.append(pl.BlockSpec(memory_space=pltpu.HBM))
    n_out = len(out_specs)

    def body(where_ref, *refs):
        weights_ref = refs[count]
        outs = refs[-n_out:]
        first = where_ref[count] == 0
        for k in range(count):

            @pl.when(pl.program_id(0) == k)
            def _():
                halves = [refs[k][:, :cols], refs[k][:, cols : 2 * cols]]
                outs[0][0, 0], outs[0][1, 0] = halves
                if with_attn:
                    outs[3][0] = refs[k][:, 2 * cols :]
                product = contract_cols(jnp.concatenate(halves), weights_ref[...]).astype(jnp.bfloat16)
                outs[1][0] = jnp.where(first, product[:TB], product[TB:])
                outs[2][0] = jnp.where(first, product[TB:], product[:TB])

    return pl.pallas_call(
        body,
        out_shape=tuple(out_shape),
        grid_spec=pltpu.PrefetchScalarGridSpec(
            num_scalar_prefetch=1, grid=(count,), in_specs=in_specs, out_specs=tuple(out_specs)
        ),
        input_output_aliases=aliases,
        compiler_params=pltpu.CompilerParams(vmem_limit_bytes=60 * 2**20),
        cost_estimate=pl.CostEstimate(
            flops=4 * count * TB * cols * width,
            bytes_accessed=2 * width * cols + 4 * count * TB * (2 * cols + attn_cols + width),
            transcendentals=0,
        ),
    )(where, *operands)


def contract_rows(halves, both, halves_left, factor, tile):
    a, b = halves.shape[2], both.shape[1]
    m, n = (a, b) if halves_left else (b, a)
    half_tile, both_tile = (tile, b) if halves_left else (a, tile)
    moving = (lambda i: (0, 0, i), lambda i: (0, 0, 0, 0)) if halves_left else (lambda i: (0, 0, 0), lambda i: (0, 0, 0, i))

    def body(halves_ref, both_ref, out_ref):
        total = jnp.zeros(out_ref.shape, jnp.float32)
        for h in range(2):
            tokens = both_ref[:, h].reshape(NZ * TB, both_tile)
            pair = (halves_ref[h], tokens) if halves_left else (tokens, halves_ref[h])
            total += lax.dot_general(*pair, (((0,), (0,)), ((), ())), preferred_element_type=jnp.float32)
        out_ref[...] = total * factor

    return pl.pallas_call(
        body,
        out_shape=jax.ShapeDtypeStruct((m, n), jnp.float32),
        grid=(m // tile,),
        in_specs=[
            pl.BlockSpec((2, NZ * TB, half_tile), moving[0]),
            pl.BlockSpec((NZ, 2, TB, both_tile), moving[1]),
        ],
        out_specs=pl.BlockSpec((tile, n), lambda i: (i, 0)),
        compiler_params=pltpu.CompilerParams(vmem_limit_bytes=40 * 2**20),
        cost_estimate=pl.CostEstimate(
            flops=4 * NZ * TB * m * n, bytes_accessed=4 * NZ * TB * (m + n) + 4 * m * n, transcendentals=0
        ),
    )(halves, both.reshape(NZ, 2, TB, b))


def chip_parts(kept, sent, targets):
    n = kept.shape[2]
    count = len(targets)
    pair = pl.BlockSpec((2, TB, n), lambda i, s: (s[i], 0, 0))

    def body(where_ref, kept_ref, sent_ref, *outs):
        total = (kept_ref[...].astype(jnp.float32) + sent_ref[...].astype(jnp.float32)).astype(jnp.bfloat16)
        for k in range(count):

            @pl.when(pl.program_id(0) == k)
            def _():
                outs[k][...] = total.reshape(2 * TB, n)

    return pl.pallas_call(
        body,
        out_shape=(jax.ShapeDtypeStruct((2 * TB, n), jnp.bfloat16),) * count,
        grid_spec=pltpu.PrefetchScalarGridSpec(
            num_scalar_prefetch=1,
            grid=(count,),
            in_specs=[pair, pair],
            out_specs=(pl.BlockSpec((2 * TB, n), lambda i, s: (0, 0)),) * count,
        ),
        cost_estimate=pl.CostEstimate(flops=NZ * TB * n, bytes_accessed=6 * NZ * TB * n, transcendentals=0),
    )(jnp.stack(targets).astype(jnp.int32), kept, sent)


def contract_cols(left, right):
    return lax.dot_general(
        left, right, (((1,), (1,)), ((), ())), preferred_element_type=jnp.float32
    )


class Fold:
    def __init__(self, partial, z):
        self.partial, self.z = partial, z
        self.rows = partial.shape[0] // NZ
        self.up = self.down = None
        self.k = 4

    def mine(self, at):
        return lax.dynamic_slice_in_dim(self.partial, at % NZ * self.rows, self.rows, 0).astype(jnp.float32)

    def add(self, part, got):
        return (part if got is None else part + got.astype(jnp.float32)).astype(jnp.bfloat16)

    def step(self):
        k = self.k
        self.k -= 1
        if k < 4:
            self.up = over_z(self.add(self.mine(self.z + k), self.up), 1)
        self.down = over_z(self.add(self.mine(self.z - k + NZ), self.down), -1)

    def sums(self):
        return self.mine(self.z) + self.up.astype(jnp.float32) + self.down.astype(jnp.float32)


def shards(inputs, out_grad, attn_out, qkv_grad, w_qkv, w_out, doc_ids):
    d, t = lax.axis_index("dp"), lax.axis_index("tensor")
    z, yh = d // 2, d % 2
    x, yl, core = t // 4, t // 2 % 2, t % 2
    factor = 1.0 / math.sqrt(NZ * 2 * TB)

    g_all = lax.all_gather(out_grad, "tensor", axis=0, tiled=True)
    x_all = lax.all_gather(inputs, "tensor", axis=0, tiled=True)

    ids = doc_ids[None, :]
    other_ids = over_yh(ids)
    q_other = over_yh(qkv_grad)
    pair_ids = jnp.where(yh == 1, jnp.concatenate([other_ids, ids]), jnp.concatenate([ids, other_ids]))
    near = [over_z(pair_ids, 1), over_z(pair_ids, 2)]
    attn, _ = tie(attn_out, pair_ids)
    up_attn, down_attn = over_z(attn, 1), over_z(attn, -1)
    far = over_z(jnp.concatenate(near), 2)
    window = jnp.concatenate([pair_ids, *near, far]).reshape(-1)
    tables = rotary_tables(pair_ids.reshape(-1), window, z)

    up0, down0 = unrotate(qkv_grad, q_other, tables, up_attn, down_attn, yh, t)
    up1, down1 = tie(over_z(up0, 1), over_z(down0, -1))

    attn_all = place_first(attn_out, z)
    *shares, attn_all = absorb([up0, down0], [0, 0], [-1, 1], z, core, w_qkv, [None, None, None, attn_all])
    *shares, attn_all = absorb([up1, down1], [-1, 1], [-2, 2], z, core, w_qkv, [*shares, attn_all])
    up2, down2, attn_all, *shares = tie(over_z(up1, 1), over_z(down1, -1), attn_all, *shares)

    *shares, attn_all = absorb([up2, down2], [-2, 2], [-3, 3], z, core, w_qkv, [*shares, attn_all])
    attn_part = contract_cols(g_all, w_out).astype(jnp.bfloat16)
    up3, down3, attn_part, attn_all, *shares = tie(over_z(up2, 1), over_z(down2, -1), attn_part, attn_all, *shares)

    fold = Fold(attn_part, z)
    fold.step()
    last = over_z(up3[:, : 2 * qkv_grad.shape[1]], 1)
    *shares, attn_all = absorb([up3, down3], [-3, 3], [4, 4], z, core, w_qkv, [*shares, attn_all])
    last, fold.down, attn_all, *shares = tie(last, fold.down, attn_all, *shares)
    attn_all = lax.all_gather(
        attn_all.reshape(1, NZ * TB, -1), "dp", axis=0, tiled=True, axis_index_groups=[[d, d + 1] for d in range(0, 16, 2)]
    )
    q_all, kept, given = absorb([last], [4], None, z, core, w_qkv, shares)

    q_all = q_all.reshape(2, NZ * TB, -1)
    sent = over_core(given)
    fold.step()
    steps = (1, -1, 2)
    mine, *away = chip_parts(kept, sent, [(x + k + NX) % NX for k in (0, *steps)])
    fold.up, fold.down, x_all, _ = tie(fold.up, fold.down, x_all, mine)
    fold.step()
    wqkv_grad = contract_rows(q_all, x_all, False, factor, 256)
    *came, wqkv_grad = tie(*(over_x(part, k) for k, part in zip(steps, away)), wqkv_grad)
    total = mine.astype(jnp.float32)
    for part in came:
        total = total + part.astype(jnp.float32)
    keep = lax.dynamic_slice_in_dim(total, yl * TB, TB, 0)
    give = lax.dynamic_slice_in_dim(total, (1 - yl) * TB, TB, 0).astype(jnp.bfloat16)
    summed = keep + over_yl(give).astype(jnp.float32)
    input_grad = (out_grad.astype(jnp.float32) + summed).astype(jnp.bfloat16)

    fold.step()
    sums = fold.sums()
    keep = lax.dynamic_slice_in_dim(sums, yh * TB, TB, 0)
    send = lax.dynamic_slice_in_dim(sums, (1 - yh) * TB, TB, 0).astype(jnp.bfloat16)
    attn_grad = (keep + over_yh(send).astype(jnp.float32)).astype(jnp.bfloat16)

    attn_all, _, _ = tie(attn_all, give, send)
    wout_grad = contract_rows(attn_all, g_all, True, factor, 256)
    return (input_grad, attn_grad, wqkv_grad, wout_grad)


def solution(mesh):
    return jax.shard_map(
        shards,
        mesh=mesh,
        in_specs=(
            P("tensor", "dp"),
            P("tensor", "dp"),
            P("dp", "tensor"),
            P("dp", "tensor"),
            P("dp", "tensor"),
            P("tensor", "dp"),
            P("dp"),
        ),
        out_specs=(P("tensor", "dp"), P("dp", "tensor"), P("dp", "tensor"), P("tensor", "dp")),
        check_vma=False,
    )
```

```python
import math

import jax
import jax.numpy as jnp
from jax import lax
from jax.experimental import pallas as pl
from jax.experimental.pallas import tpu as pltpu
from jax.sharding import PartitionSpec as P

HD = 128
HQ = 96
HK = 8
ROPE_BASE = 500000.0
NZ = 8
NX = 4
TB = 128
BEHIND = 4


def over_z(value, steps):
    pairs = [(z * 2 + h, (z + steps) % NZ * 2 + h) for z in range(NZ) for h in range(2)]
    return lax.ppermute(value, "dp", pairs)


def over_yh(value):
    return lax.ppermute(value, "dp", [(d, d ^ 1) for d in range(16)])


def over_x(value, steps):
    pairs = [(x * 4 + k, (x + steps) % NX * 4 + k) for x in range(NX) for k in range(4)]
    return lax.ppermute(value, "tensor", pairs)


def over_yl(value):
    return lax.ppermute(value, "tensor", [(t, t ^ 2) for t in range(16)])


def over_core(value):
    return lax.ppermute(value, "tensor", [(t, t ^ 1) for t in range(16)])


def tie(*values):
    return lax.optimization_barrier(values)


def rotary_tables(ids, window, z):
    smaller = jnp.sum((window[None, :] < ids[:, None]).astype(jnp.int32), axis=1)
    start = jnp.maximum((z - BEHIND) * 2 * TB, 0) + smaller
    positions = z * 2 * TB + jnp.arange(2 * TB, dtype=jnp.int32) - start
    lane = jnp.arange(HD, dtype=jnp.int32)
    frequency = jnp.power(jnp.float32(ROPE_BASE), -(2.0 * (lane // 2).astype(jnp.float32)) / HD)
    angles = positions.astype(jnp.float32)[:, None] * frequency[None, :]
    sign = jnp.where(lane % 2 == 0, 1.0, -1.0)
    return jnp.cos(angles), jnp.sin(angles) * sign[None, :]


def unrotate_kernel(where_ref, own_ref, other_ref, cos_ref, sin_ref, up_attn_ref, down_attn_ref, up_ref, down_ref):
    even = lax.broadcasted_iota(jnp.int32, (TB, HD), 1) % 2 == 0
    swapped = where_ref[0] == 1
    cols = own_ref.shape[1]
    for h in range(cols // HD):
        part = slice(h * HD, (h + 1) * HD)
        rotated = where_ref[1] + h < HQ + HK
        own, other = own_ref[:, part], other_ref[:, part]
        for half in range(2):
            rows = slice(half * TB, (half + 1) * TB)
            values = jnp.where(swapped, *((other, own) if half == 0 else (own, other))).astype(jnp.float32)
            partner = jnp.where(even, pltpu.roll(values, HD - 1, 1), pltpu.roll(values, 1, 1))
            cosine = jnp.where(rotated, cos_ref[rows, :], 1.0)
            sine = jnp.where(rotated, sin_ref[rows, :], 0.0)
            result = (values * cosine + partner * sine).astype(jnp.bfloat16)
            at = slice(half * cols + h * HD, half * cols + (h + 1) * HD)
            up_ref[:, at] = result
            down_ref[:, at] = result
    up_ref[:, 2 * cols :] = up_attn_ref[...]
    down_ref[:, 2 * cols :] = down_attn_ref[...]


def unrotate(own, other, tables, up_attn, down_attn, yh, t):
    cols = own.shape[1]
    vmem = pl.BlockSpec(memory_space=pltpu.VMEM)
    shape = jax.ShapeDtypeStruct((TB, 2 * cols + up_attn.shape[1]), jnp.bfloat16)
    return pl.pallas_call(
        unrotate_kernel,
        out_shape=(shape, shape),
        in_specs=[pl.BlockSpec(memory_space=pltpu.SMEM)] + [vmem] * 6,
        out_specs=(vmem, vmem),
        cost_estimate=pl.CostEstimate(flops=20 * TB * cols, bytes_accessed=16 * TB * cols, transcendentals=0),
    )(jnp.stack([yh, t * (cols // HD)]).astype(jnp.int32), own, other, *tables, up_attn, down_attn)


def place_first(block, z):
    def body(z_ref, block_ref, out_ref):
        out_ref[0] = block_ref[...]

    n = block.shape[1]
    return pl.pallas_call(
        body,
        out_shape=jax.ShapeDtypeStruct((NZ, TB, n), jnp.bfloat16),
        grid_spec=pltpu.PrefetchScalarGridSpec(
            num_scalar_prefetch=1,
            grid=(1,),
            in_specs=[pl.BlockSpec((TB, n), lambda i, s: (0, 0))],
            out_specs=pl.BlockSpec((1, TB, n), lambda i, s: (s[0], 0, 0)),
        ),
    )(jnp.reshape(z, (1,)).astype(jnp.int32), block)


def absorb(blocks, q_places, a_places, z, core, weights, wholes):
    count, with_attn = len(blocks), bool(a_places)
    width, cols = weights.shape
    attn_cols = blocks[0].shape[1] - 2 * cols
    at = lambda p: (z + p + NZ) % NZ
    where = jnp.stack([*map(at, q_places), core, *map(at, a_places or ())]).astype(jnp.int32)
    q_spec = pl.BlockSpec((2, 1, TB, cols), lambda i, s: (0, s[i], 0, 0))
    share = pl.BlockSpec((1, TB, width), lambda i, s: (s[i], 0, 0))
    out_specs = [q_spec, share, share]
    out_shape = [jax.ShapeDtypeStruct((2, NZ, TB, cols), jnp.bfloat16)]
    out_shape += [jax.ShapeDtypeStruct((NZ, TB, width), jnp.bfloat16)] * 2
    if with_attn:
        out_specs.append(pl.BlockSpec((1, TB, attn_cols), lambda i, s: (s[count + 1 + i], 0, 0)))
        out_shape.append(jax.ShapeDtypeStruct((NZ, TB, attn_cols), jnp.bfloat16))
    operands = [*blocks, weights]
    in_specs = [pl.BlockSpec(v.shape, lambda i, s: (0, 0)) for v in operands]
    aliases = {}
    for k, whole in enumerate(wholes):
        if whole is not None:
            aliases[1 + len(operands)] = k
            operands.append(whole)
            in_specs.append(pl.BlockSpec(memory_space=pltpu.HBM))
    n_out = len(out_specs)

    def body(where_ref, *refs):
        weights_ref = refs[count]
        outs = refs[-n_out:]
        first = where_ref[count] == 0
        for k in range(count):

            @pl.when(pl.program_id(0) == k)
            def _():
                halves = [refs[k][:, :cols], refs[k][:, cols : 2 * cols]]
                outs[0][0, 0], outs[0][1, 0] = halves
                if with_attn:
                    outs[3][0] = refs[k][:, 2 * cols :]
                product = contract_cols(jnp.concatenate(halves), weights_ref[...]).astype(jnp.bfloat16)
                outs[1][0] = jnp.where(first, product[:TB], product[TB:])
                outs[2][0] = jnp.where(first, product[TB:], product[:TB])

    return pl.pallas_call(
        body,
        out_shape=tuple(out_shape),
        grid_spec=pltpu.PrefetchScalarGridSpec(
            num_scalar_prefetch=1, grid=(count,), in_specs=in_specs, out_specs=tuple(out_specs)
        ),
        input_output_aliases=aliases,
        compiler_params=pltpu.CompilerParams(vmem_limit_bytes=60 * 2**20),
        cost_estimate=pl.CostEstimate(
            flops=4 * count * TB * cols * width,
            bytes_accessed=2 * width * cols + 4 * count * TB * (2 * cols + attn_cols + width),
            transcendentals=0,
        ),
    )(where, *operands)


def chip_parts(kept, sent, targets):
    n = kept.shape[2]
    count = len(targets)
    pair = pl.BlockSpec((2, TB, n), lambda i, s: (s[i], 0, 0))

    def body(where_ref, kept_ref, sent_ref, *outs):
        total = (kept_ref[...].astype(jnp.float32) + sent_ref[...].astype(jnp.float32)).astype(jnp.bfloat16)
        for k in range(count):

            @pl.when(pl.program_id(0) == k)
            def _():
                outs[k][...] = total.reshape(2 * TB, n)

    return pl.pallas_call(
        body,
        out_shape=(jax.ShapeDtypeStruct((2 * TB, n), jnp.bfloat16),) * count,
        grid_spec=pltpu.PrefetchScalarGridSpec(
            num_scalar_prefetch=1,
            grid=(count,),
            in_specs=[pair, pair],
            out_specs=(pl.BlockSpec((2 * TB, n), lambda i, s: (0, 0)),) * count,
        ),
        cost_estimate=pl.CostEstimate(flops=NZ * TB * n, bytes_accessed=6 * NZ * TB * n, transcendentals=0),
    )(jnp.stack(targets).astype(jnp.int32), kept, sent)


def contract_rows(halves, first, both, halves_left, factor, tile):
    a, b = halves[0].shape[2], both.shape[1]
    m, n = (a, b) if halves_left else (b, a)
    half_tile, both_tile = (tile, b) if halves_left else (a, tile)
    if halves_left:
        moving = (lambda i, s: (0, 0, i), lambda i, s: (0, 0, 0, 0))
    else:
        moving = (lambda i, s: (0, 0, 0), lambda i, s: (0, 0, 0, i))

    def body(first_ref, *refs):
        both_ref, out_ref = refs[-2:]
        total = jnp.zeros(out_ref.shape, jnp.float32)
        parts = [ref[k] for ref in refs[:-2] for k in range(ref.shape[0])]
        for part, h in zip(parts, (first_ref[0], 1 - first_ref[0])):
            tokens = both_ref[:, h].reshape(NZ * TB, both_tile)
            pair = (part, tokens) if halves_left else (tokens, part)
            total += lax.dot_general(*pair, (((0,), (0,)), ((), ())), preferred_element_type=jnp.float32)
        out_ref[...] = total * factor

    return pl.pallas_call(
        body,
        out_shape=jax.ShapeDtypeStruct((m, n), jnp.float32),
        grid_spec=pltpu.PrefetchScalarGridSpec(
            num_scalar_prefetch=1,
            grid=(m // tile,),
            in_specs=[pl.BlockSpec((v.shape[0], NZ * TB, half_tile), moving[0]) for v in halves]
            + [pl.BlockSpec((NZ, 2, TB, both_tile), moving[1])],
            out_specs=pl.BlockSpec((tile, n), lambda i, s: (i, 0)),
        ),
        compiler_params=pltpu.CompilerParams(vmem_limit_bytes=40 * 2**20),
        cost_estimate=pl.CostEstimate(
            flops=4 * NZ * TB * m * n, bytes_accessed=4 * NZ * TB * (m + n) + 4 * m * n, transcendentals=0
        ),
    )(jnp.reshape(first, (1,)).astype(jnp.int32), *halves, both.reshape(NZ, 2, TB, b))


def contract_cols(left, right):
    return lax.dot_general(
        left, right, (((1,), (1,)), ((), ())), preferred_element_type=jnp.float32
    )


class Fold:
    def __init__(self, partial, z):
        self.partial, self.z = partial, z
        self.rows = partial.shape[0] // NZ
        self.up = self.down = None
        self.k = 4

    def mine(self, at):
        return lax.dynamic_slice_in_dim(self.partial, at % NZ * self.rows, self.rows, 0).astype(jnp.float32)

    def add(self, part, got):
        return (part if got is None else part + got.astype(jnp.float32)).astype(jnp.bfloat16)

    def step(self):
        k = self.k
        self.k -= 1
        if k < 4:
            self.up = over_z(self.add(self.mine(self.z + k), self.up), 1)
        self.down = over_z(self.add(self.mine(self.z - k + NZ), self.down), -1)

    def sums(self):
        return self.mine(self.z) + self.up.astype(jnp.float32) + self.down.astype(jnp.float32)


def shards(inputs, out_grad, attn_out, qkv_grad, w_qkv, w_out, doc_ids):
    d, t = lax.axis_index("dp"), lax.axis_index("tensor")
    z, yh = d // 2, d % 2
    x, yl, core = t // 4, t // 2 % 2, t % 2
    factor = 1.0 / math.sqrt(NZ * 2 * TB)

    g_all = lax.all_gather(out_grad, "tensor", axis=0, tiled=True)
    x_all = lax.all_gather(inputs, "tensor", axis=0, tiled=True)

    ids = doc_ids[None, :]
    other_ids = over_yh(ids)
    q_other = over_yh(qkv_grad)
    pair_ids = jnp.where(yh == 1, jnp.concatenate([other_ids, ids]), jnp.concatenate([ids, other_ids]))
    near = [over_z(pair_ids, 1), over_z(pair_ids, 2)]
    attn, _ = tie(attn_out, pair_ids)
    up_attn, down_attn = over_z(attn, 1), over_z(attn, -1)
    far = over_z(jnp.concatenate(near), 2)
    window = jnp.concatenate([pair_ids, *near, far]).reshape(-1)
    tables = rotary_tables(pair_ids.reshape(-1), window, z)

    up0, down0 = unrotate(qkv_grad, q_other, tables, up_attn, down_attn, yh, t)
    up1, down1 = tie(over_z(up0, 1), over_z(down0, -1))

    attn_all = place_first(attn_out, z)
    *shares, attn_all = absorb([up0, down0], [0, 0], [-1, 1], z, core, w_qkv, [None, None, None, attn_all])
    *shares, attn_all = absorb([up1, down1], [-1, 1], [-2, 2], z, core, w_qkv, [*shares, attn_all])
    up2, down2, attn_all, *shares = tie(over_z(up1, 1), over_z(down1, -1), attn_all, *shares)

    *shares, attn_all = absorb([up2, down2], [-2, 2], [-3, 3], z, core, w_qkv, [*shares, attn_all])
    attn_part = contract_cols(g_all, w_out).astype(jnp.bfloat16)
    up3, down3, attn_part, attn_all, *shares = tie(over_z(up2, 1), over_z(down2, -1), attn_part, attn_all, *shares)

    fold = Fold(attn_part, z)
    fold.step()
    last = over_z(up3[:, : 2 * qkv_grad.shape[1]], 1)
    *shares, attn_all = absorb([up3, down3], [-3, 3], [4, 4], z, core, w_qkv, [*shares, attn_all])
    last, fold.down, attn_all, *shares = tie(last, fold.down, attn_all, *shares)
    q_all, kept, given = absorb([last], [4], None, z, core, w_qkv, shares)

    q_all = q_all.reshape(2, NZ * TB, -1)
    sent = over_core(given)
    attn_all = attn_all.reshape(1, NZ * TB, -1)
    attn_other = over_yh(attn_all)
    fold.step()
    mine, ahead, behind, across = chip_parts(kept, sent, [(x + k) % NX for k in (0, 1, 3, 2)])
    fold.up, fold.down, x_all, _ = tie(fold.up, fold.down, x_all, mine)
    fold.step()
    a, b = over_x(across[:TB], 1), over_x(across[TB:], -1)
    plus = lambda part, got: (part.astype(jnp.float32) + got.astype(jnp.float32)).astype(jnp.bfloat16)
    ahead = jnp.concatenate([plus(ahead[:TB], a), ahead[TB:]])
    behind = jnp.concatenate([behind[:TB], plus(behind[TB:], b)])
    ahead, behind = tie(ahead, behind)
    wqkv_grad = contract_rows([q_all], jnp.int32(0), x_all, False, factor, 256)
    came1, came2 = over_x(ahead, 1), over_x(behind, -1)
    total = mine.astype(jnp.float32) + came1.astype(jnp.float32) + came2.astype(jnp.float32)
    keep = lax.dynamic_slice_in_dim(total, yl * TB, TB, 0)
    give = lax.dynamic_slice_in_dim(total, (1 - yl) * TB, TB, 0).astype(jnp.bfloat16)
    summed = keep + over_yl(give).astype(jnp.float32)
    input_grad = (out_grad.astype(jnp.float32) + summed).astype(jnp.bfloat16)

    fold.up, fold.down, attn_other, wqkv_grad, _ = tie(fold.up, fold.down, attn_other, wqkv_grad, ahead)
    fold.step()
    wout_grad = contract_rows([attn_all, attn_other], yh, g_all, True, factor, 256)
    fold.up, fold.down, wout_grad = tie(fold.up, fold.down, wout_grad)
    sums = fold.sums()
    keep = lax.dynamic_slice_in_dim(sums, yh * TB, TB, 0)
    send = lax.dynamic_slice_in_dim(sums, (1 - yh) * TB, TB, 0).astype(jnp.bfloat16)
    attn_grad = (keep + over_yh(send).astype(jnp.float32)).astype(jnp.bfloat16)

    return (input_grad, attn_grad, wqkv_grad, wout_grad)


def solution(mesh):
    return jax.shard_map(
        shards,
        mesh=mesh,
        in_specs=(
            P("tensor", "dp"),
            P("tensor", "dp"),
            P("dp", "tensor"),
            P("dp", "tensor"),
            P("dp", "tensor"),
            P("tensor", "dp"),
            P("dp"),
        ),
        out_specs=(P("tensor", "dp"), P("dp", "tensor"), P("dp", "tensor"), P("tensor", "dp")),
        check_vma=False,
    )
```

```python
import math

import jax
import jax.numpy as jnp
from jax import lax
from jax.experimental import pallas as pl
from jax.experimental.pallas import tpu as pltpu
from jax.sharding import PartitionSpec as P

HD = 128
HQ = 96
HK = 8
ROPE_BASE = 500000.0
NZ = 8
NX = 4
TB = 128
BEHIND = 4


def over_z(value, steps):
    pairs = [(z * 2 + h, (z + steps) % NZ * 2 + h) for z in range(NZ) for h in range(2)]
    return lax.ppermute(value, "dp", pairs)


def over_yh(value):
    return lax.ppermute(value, "dp", [(d, d ^ 1) for d in range(16)])


def over_x(value, steps):
    pairs = [(x * 4 + k, (x + steps) % NX * 4 + k) for x in range(NX) for k in range(4)]
    return lax.ppermute(value, "tensor", pairs)


def over_yl(value):
    return lax.ppermute(value, "tensor", [(t, t ^ 2) for t in range(16)])


def over_core(value):
    return lax.ppermute(value, "tensor", [(t, t ^ 1) for t in range(16)])


def tie(*values):
    return lax.optimization_barrier(values)


def rotary_tables(ids, window, z):
    smaller = jnp.sum((window[None, :] < ids[:, None]).astype(jnp.int32), axis=1)
    start = jnp.maximum((z - BEHIND) * 2 * TB, 0) + smaller
    positions = z * 2 * TB + jnp.arange(2 * TB, dtype=jnp.int32) - start
    lane = jnp.arange(HD, dtype=jnp.int32)
    frequency = jnp.power(jnp.float32(ROPE_BASE), -(2.0 * (lane // 2).astype(jnp.float32)) / HD)
    angles = positions.astype(jnp.float32)[:, None] * frequency[None, :]
    sign = jnp.where(lane % 2 == 0, 1.0, -1.0)
    return jnp.cos(angles), jnp.sin(angles) * sign[None, :]


def unrotate_kernel(where_ref, own_ref, other_ref, cos_ref, sin_ref, up_attn_ref, down_attn_ref, up_ref, down_ref):
    even = lax.broadcasted_iota(jnp.int32, (TB, HD), 1) % 2 == 0
    swapped = where_ref[0] == 1
    cols = own_ref.shape[1]
    for h in range(cols // HD):
        part = slice(h * HD, (h + 1) * HD)
        rotated = where_ref[1] + h < HQ + HK
        own, other = own_ref[:, part], other_ref[:, part]
        for half in range(2):
            rows = slice(half * TB, (half + 1) * TB)
            values = jnp.where(swapped, *((other, own) if half == 0 else (own, other))).astype(jnp.float32)
            partner = jnp.where(even, pltpu.roll(values, HD - 1, 1), pltpu.roll(values, 1, 1))
            cosine = jnp.where(rotated, cos_ref[rows, :], 1.0)
            sine = jnp.where(rotated, sin_ref[rows, :], 0.0)
            result = (values * cosine + partner * sine).astype(jnp.bfloat16)
            at = slice(half * cols + h * HD, half * cols + (h + 1) * HD)
            up_ref[:, at] = result
            down_ref[:, at] = result
    up_ref[:, 2 * cols :] = up_attn_ref[...]
    down_ref[:, 2 * cols :] = down_attn_ref[...]


def unrotate(own, other, tables, up_attn, down_attn, yh, t):
    cols = own.shape[1]
    vmem = pl.BlockSpec(memory_space=pltpu.VMEM)
    shape = jax.ShapeDtypeStruct((TB, 2 * cols + up_attn.shape[1]), jnp.bfloat16)
    return pl.pallas_call(
        unrotate_kernel,
        out_shape=(shape, shape),
        in_specs=[pl.BlockSpec(memory_space=pltpu.SMEM)] + [vmem] * 6,
        out_specs=(vmem, vmem),
        cost_estimate=pl.CostEstimate(flops=20 * TB * cols, bytes_accessed=16 * TB * cols, transcendentals=0),
    )(jnp.stack([yh, t * (cols // HD)]).astype(jnp.int32), own, other, *tables, up_attn, down_attn)


def place_first(block, z):
    def body(z_ref, block_ref, out_ref):
        out_ref[0] = block_ref[...]

    n = block.shape[1]
    return pl.pallas_call(
        body,
        out_shape=jax.ShapeDtypeStruct((NZ, TB, n), jnp.bfloat16),
        grid_spec=pltpu.PrefetchScalarGridSpec(
            num_scalar_prefetch=1,
            grid=(1,),
            in_specs=[pl.BlockSpec((TB, n), lambda i, s: (0, 0))],
            out_specs=pl.BlockSpec((1, TB, n), lambda i, s: (s[0], 0, 0)),
        ),
    )(jnp.reshape(z, (1,)).astype(jnp.int32), block)


def absorb(blocks, q_places, a_places, z, core, weights, wholes):
    count, with_attn = len(blocks), bool(a_places)
    width, cols = weights.shape
    attn_cols = blocks[0].shape[1] - 2 * cols
    at = lambda p: (z + p + NZ) % NZ
    where = jnp.stack([*map(at, q_places), core, *map(at, a_places or ())]).astype(jnp.int32)
    q_spec = pl.BlockSpec((2, 1, TB, cols), lambda i, s: (0, s[i], 0, 0))
    share = pl.BlockSpec((1, TB, width), lambda i, s: (s[i], 0, 0))
    out_specs = [q_spec, share, share]
    out_shape = [jax.ShapeDtypeStruct((2, NZ, TB, cols), jnp.bfloat16)]
    out_shape += [jax.ShapeDtypeStruct((NZ, TB, width), jnp.bfloat16)] * 2
    if with_attn:
        out_specs.append(pl.BlockSpec((1, TB, attn_cols), lambda i, s: (s[count + 1 + i], 0, 0)))
        out_shape.append(jax.ShapeDtypeStruct((NZ, TB, attn_cols), jnp.bfloat16))
    operands = [*blocks, weights]
    in_specs = [pl.BlockSpec(v.shape, lambda i, s: (0, 0)) for v in operands]
    aliases = {}
    for k, whole in enumerate(wholes):
        if whole is not None:
            aliases[1 + len(operands)] = k
            operands.append(whole)
            in_specs.append(pl.BlockSpec(memory_space=pltpu.HBM))
    n_out = len(out_specs)

    def body(where_ref, *refs):
        weights_ref = refs[count]
        outs = refs[-n_out:]
        first = where_ref[count] == 0
        for k in range(count):

            @pl.when(pl.program_id(0) == k)
            def _():
                halves = [refs[k][:, :cols], refs[k][:, cols : 2 * cols]]
                outs[0][0, 0], outs[0][1, 0] = halves
                if with_attn:
                    outs[3][0] = refs[k][:, 2 * cols :]
                product = contract_cols(jnp.concatenate(halves), weights_ref[...]).astype(jnp.bfloat16)
                outs[1][0] = jnp.where(first, product[:TB], product[TB:])
                outs[2][0] = jnp.where(first, product[TB:], product[:TB])

    return pl.pallas_call(
        body,
        out_shape=tuple(out_shape),
        grid_spec=pltpu.PrefetchScalarGridSpec(
            num_scalar_prefetch=1, grid=(count,), in_specs=in_specs, out_specs=tuple(out_specs)
        ),
        input_output_aliases=aliases,
        compiler_params=pltpu.CompilerParams(vmem_limit_bytes=60 * 2**20),
        cost_estimate=pl.CostEstimate(
            flops=4 * count * TB * cols * width,
            bytes_accessed=2 * width * cols + 4 * count * TB * (2 * cols + attn_cols + width),
            transcendentals=0,
        ),
    )(where, *operands)


def chip_parts(kept, sent, targets):
    n = kept.shape[2]
    count = len(targets)
    pair = pl.BlockSpec((2, TB, n), lambda i, s: (s[i], 0, 0))

    def body(where_ref, kept_ref, sent_ref, *outs):
        total = (kept_ref[...].astype(jnp.float32) + sent_ref[...].astype(jnp.float32)).astype(jnp.bfloat16)
        for k in range(count):

            @pl.when(pl.program_id(0) == k)
            def _():
                outs[k][...] = total.reshape(2 * TB, n)

    return pl.pallas_call(
        body,
        out_shape=(jax.ShapeDtypeStruct((2 * TB, n), jnp.bfloat16),) * count,
        grid_spec=pltpu.PrefetchScalarGridSpec(
            num_scalar_prefetch=1,
            grid=(count,),
            in_specs=[pair, pair],
            out_specs=(pl.BlockSpec((2 * TB, n), lambda i, s: (0, 0)),) * count,
        ),
        cost_estimate=pl.CostEstimate(flops=NZ * TB * n, bytes_accessed=6 * NZ * TB * n, transcendentals=0),
    )(jnp.stack(targets).astype(jnp.int32), kept, sent)


def contract_rows(halves, first, both, halves_left, factor, tile):
    a, b = halves[0].shape[2], both.shape[1]
    m, n = (a, b) if halves_left else (b, a)
    half_tile, both_tile = (tile, b) if halves_left else (a, tile)
    if halves_left:
        moving = (lambda i, s: (0, 0, i), lambda i, s: (0, 0, 0, 0))
    else:
        moving = (lambda i, s: (0, 0, 0), lambda i, s: (0, 0, 0, i))

    def body(first_ref, *refs):
        both_ref, out_ref = refs[-2:]
        total = jnp.zeros(out_ref.shape, jnp.float32)
        parts = [ref[k] for ref in refs[:-2] for k in range(ref.shape[0])]
        for part, h in zip(parts, (first_ref[0], 1 - first_ref[0])):
            tokens = both_ref[:, h].reshape(NZ * TB, both_tile)
            pair = (part, tokens) if halves_left else (tokens, part)
            total += lax.dot_general(*pair, (((0,), (0,)), ((), ())), preferred_element_type=jnp.float32)
        out_ref[...] = total * factor

    return pl.pallas_call(
        body,
        out_shape=jax.ShapeDtypeStruct((m, n), jnp.float32),
        grid_spec=pltpu.PrefetchScalarGridSpec(
            num_scalar_prefetch=1,
            grid=(m // tile,),
            in_specs=[pl.BlockSpec((v.shape[0], NZ * TB, half_tile), moving[0]) for v in halves]
            + [pl.BlockSpec((NZ, 2, TB, both_tile), moving[1])],
            out_specs=pl.BlockSpec((tile, n), lambda i, s: (i, 0)),
        ),
        compiler_params=pltpu.CompilerParams(vmem_limit_bytes=40 * 2**20),
        cost_estimate=pl.CostEstimate(
            flops=4 * NZ * TB * m * n, bytes_accessed=4 * NZ * TB * (m + n) + 4 * m * n, transcendentals=0
        ),
    )(jnp.reshape(first, (1,)).astype(jnp.int32), *halves, both.reshape(NZ, 2, TB, b))


def contract_cols(left, right):
    return lax.dot_general(
        left, right, (((1,), (1,)), ((), ())), preferred_element_type=jnp.float32
    )


class Fold:
    def __init__(self, partial, z):
        self.partial, self.z = partial, z
        self.rows = partial.shape[0] // NZ
        self.up = self.down = None
        self.k = 4

    def mine(self, at):
        return lax.dynamic_slice_in_dim(self.partial, at % NZ * self.rows, self.rows, 0).astype(jnp.float32)

    def add(self, part, got):
        return (part if got is None else part + got.astype(jnp.float32)).astype(jnp.bfloat16)

    def step(self):
        k = self.k
        self.k -= 1
        if k < 4:
            self.up = over_z(self.add(self.mine(self.z + k), self.up), 1)
        self.down = over_z(self.add(self.mine(self.z - k + NZ), self.down), -1)

    def sums(self):
        return self.mine(self.z) + self.up.astype(jnp.float32) + self.down.astype(jnp.float32)


def shards(inputs, out_grad, attn_out, qkv_grad, w_qkv, w_out, doc_ids):
    d, t = lax.axis_index("dp"), lax.axis_index("tensor")
    z, yh = d // 2, d % 2
    x, yl, core = t // 4, t // 2 % 2, t % 2
    factor = 1.0 / math.sqrt(NZ * 2 * TB)

    g_all = lax.all_gather(out_grad, "tensor", axis=0, tiled=True)
    x_all = lax.all_gather(inputs, "tensor", axis=0, tiled=True)

    ids = doc_ids[None, :]
    other_ids = over_yh(ids)
    q_other = over_yh(qkv_grad)
    pair_ids = jnp.where(yh == 1, jnp.concatenate([other_ids, ids]), jnp.concatenate([ids, other_ids]))
    near = [over_z(pair_ids, 1), over_z(pair_ids, 2)]
    attn, _ = tie(attn_out, pair_ids)
    up_attn, down_attn = over_z(attn, 1), over_z(attn, -1)
    far = over_z(jnp.concatenate(near), 2)
    window = jnp.concatenate([pair_ids, *near, far]).reshape(-1)
    tables = rotary_tables(pair_ids.reshape(-1), window, z)

    up0, down0 = unrotate(qkv_grad, q_other, tables, up_attn, down_attn, yh, t)
    up1, down1 = tie(over_z(up0, 1), over_z(down0, -1))

    attn_all = place_first(attn_out, z)
    *shares, attn_all = absorb([up0, down0], [0, 0], [-1, 1], z, core, w_qkv, [None, None, None, attn_all])
    *shares, attn_all = absorb([up1, down1], [-1, 1], [-2, 2], z, core, w_qkv, [*shares, attn_all])
    up2, down2, attn_all, *shares = tie(over_z(up1, 1), over_z(down1, -1), attn_all, *shares)

    *shares, attn_all = absorb([up2, down2], [-2, 2], [-3, 3], z, core, w_qkv, [*shares, attn_all])
    attn_part = contract_cols(g_all, w_out).astype(jnp.bfloat16)
    up3, down3, attn_part, attn_all, *shares = tie(over_z(up2, 1), over_z(down2, -1), attn_part, attn_all, *shares)

    fold = Fold(attn_part, z)
    fold.step()
    last = over_z(up3[:, : 2 * qkv_grad.shape[1]], 1)
    *shares, attn_all = absorb([up3, down3], [-3, 3], [4, 4], z, core, w_qkv, [*shares, attn_all])
    last, fold.down, attn_all, *shares = tie(last, fold.down, attn_all, *shares)
    q_all, kept, given = absorb([last], [4], None, z, core, w_qkv, shares)

    q_all = q_all.reshape(2, NZ * TB, -1)
    sent = over_core(given)
    attn_all = attn_all.reshape(1, NZ * TB, -1)
    attn_other = over_yh(attn_all)
    fold.step()
    mine, ahead, behind, across = chip_parts(kept, sent, [(x + k) % NX for k in (0, 1, 3, 2)])
    fold.up, fold.down, x_all, _ = tie(fold.up, fold.down, x_all, mine)
    fold.step()
    a, b = over_x(across[:TB], 1), over_x(across[TB:], -1)
    plus = lambda part, got: (part.astype(jnp.float32) + got.astype(jnp.float32)).astype(jnp.bfloat16)
    ahead = jnp.concatenate([plus(ahead[:TB], a), ahead[TB:]])
    behind = jnp.concatenate([behind[:TB], plus(behind[TB:], b)])
    ahead, behind = tie(ahead, behind)
    wqkv_grad = contract_rows([q_all], jnp.int32(0), x_all, False, factor, 256)
    came1, came2 = over_x(ahead, 1), over_x(behind, -1)
    came1, came2, attn_other = tie(came1, came2, attn_other)
    total = mine.astype(jnp.float32) + came1.astype(jnp.float32) + came2.astype(jnp.float32)
    keep = lax.dynamic_slice_in_dim(total, yl * TB, TB, 0)
    give = lax.dynamic_slice_in_dim(total, (1 - yl) * TB, TB, 0).astype(jnp.bfloat16)
    summed = keep + over_yl(give).astype(jnp.float32)
    input_grad = (out_grad.astype(jnp.float32) + summed).astype(jnp.bfloat16)

    fold.up, fold.down, wqkv_grad, _ = tie(fold.up, fold.down, wqkv_grad, ahead)
    fold.step()
    sums = fold.sums()
    keep = lax.dynamic_slice_in_dim(sums, yh * TB, TB, 0)
    send = lax.dynamic_slice_in_dim(sums, (1 - yh) * TB, TB, 0).astype(jnp.bfloat16)
    attn_grad = (keep + over_yh(send).astype(jnp.float32)).astype(jnp.bfloat16)

    attn_other, _, _ = tie(attn_other, give, send)
    wout_grad = contract_rows([attn_all, attn_other], yh, g_all, True, factor, 256)
    return (input_grad, attn_grad, wqkv_grad, wout_grad)


def solution(mesh):
    return jax.shard_map(
        shards,
        mesh=mesh,
        in_specs=(
            P("tensor", "dp"),
            P("tensor", "dp"),
            P("dp", "tensor"),
            P("dp", "tensor"),
            P("dp", "tensor"),
            P("tensor", "dp"),
            P("dp"),
        ),
        out_specs=(P("tensor", "dp"), P("dp", "tensor"), P("dp", "tensor"), P("tensor", "dp")),
        check_vma=False,
    )
```

```python
import math

import jax
import jax.numpy as jnp
from jax import lax
from jax.experimental import pallas as pl
from jax.experimental.pallas import tpu as pltpu
from jax.sharding import PartitionSpec as P

HD = 128
HQ = 96
HK = 8
ROPE_BASE = 500000.0
NZ = 8
NX = 4
TB = 128
Z, YH, X, CORE, T = range(5)
BEHIND = 4


def over_z(value, steps):
    pairs = [(z * 2 + h, (z + steps) % NZ * 2 + h) for z in range(NZ) for h in range(2)]
    return lax.ppermute(value, "dp", pairs)


def over_yh(value):
    return lax.ppermute(value, "dp", [(d, d ^ 1) for d in range(16)])


def over_x(value, steps):
    pairs = [(x * 4 + k, (x + steps) % NX * 4 + k) for x in range(NX) for k in range(4)]
    return lax.ppermute(value, "tensor", pairs)


def over_yl(value):
    return lax.ppermute(value, "tensor", [(t, t ^ 2) for t in range(16)])


def over_core(value):
    return lax.ppermute(value, "tensor", [(t, t ^ 1) for t in range(16)])


def tie(*values):
    return lax.optimization_barrier(values)


def rotary_tables(ids, window, z):
    smaller = jnp.sum((window[None, :] < ids[:, None]).astype(jnp.int32), axis=1)
    start = jnp.maximum((z - BEHIND) * 2 * TB, 0) + smaller
    positions = z * 2 * TB + jnp.arange(2 * TB, dtype=jnp.int32) - start
    lane = jnp.arange(HD, dtype=jnp.int32)
    frequency = jnp.power(jnp.float32(ROPE_BASE), -(2.0 * (lane // 2).astype(jnp.float32)) / HD)
    angles = positions.astype(jnp.float32)[:, None] * frequency[None, :]
    sign = jnp.where(lane % 2 == 0, 1.0, -1.0)
    return jnp.cos(angles), jnp.sin(angles) * sign[None, :]


def unrotate_kernel(where_ref, own_ref, other_ref, cos_ref, sin_ref, up_attn_ref, down_attn_ref, up_ref, down_ref):
    even = lax.broadcasted_iota(jnp.int32, (TB, HD), 1) % 2 == 0
    swapped = where_ref[YH] == 1
    cols = own_ref.shape[1]
    for h in range(cols // HD):
        part = slice(h * HD, (h + 1) * HD)
        rotated = where_ref[T] * (cols // HD) + h < HQ + HK
        own, other = own_ref[:, part], other_ref[:, part]
        for half in range(2):
            rows = slice(half * TB, (half + 1) * TB)
            values = jnp.where(swapped, *((other, own) if half == 0 else (own, other))).astype(jnp.float32)
            partner = jnp.where(even, pltpu.roll(values, HD - 1, 1), pltpu.roll(values, 1, 1))
            cosine = jnp.where(rotated, cos_ref[rows, :], 1.0)
            sine = jnp.where(rotated, sin_ref[rows, :], 0.0)
            result = (values * cosine + partner * sine).astype(jnp.bfloat16)
            at = slice(half * cols + h * HD, half * cols + (h + 1) * HD)
            up_ref[:, at] = result
            down_ref[:, at] = result
    up_ref[:, 2 * cols :] = up_attn_ref[...]
    down_ref[:, 2 * cols :] = down_attn_ref[...]


def unrotate(own, other, tables, up_attn, down_attn, spot):
    cols = own.shape[1]
    vmem = pl.BlockSpec(memory_space=pltpu.VMEM)
    shape = jax.ShapeDtypeStruct((TB, 2 * cols + up_attn.shape[1]), jnp.bfloat16)
    return pl.pallas_call(
        unrotate_kernel,
        out_shape=(shape, shape),
        in_specs=[pl.BlockSpec(memory_space=pltpu.SMEM)] + [vmem] * 6,
        out_specs=(vmem, vmem),
        cost_estimate=pl.CostEstimate(flops=20 * TB * cols, bytes_accessed=16 * TB * cols, transcendentals=0),
    )(spot, own, other, *tables, up_attn, down_attn)


def place_first(block, spot):
    def body(z_ref, block_ref, out_ref):
        out_ref[0] = block_ref[...]

    n = block.shape[1]
    return pl.pallas_call(
        body,
        out_shape=jax.ShapeDtypeStruct((NZ, TB, n), jnp.bfloat16),
        grid_spec=pltpu.PrefetchScalarGridSpec(
            num_scalar_prefetch=1,
            grid=(1,),
            in_specs=[pl.BlockSpec((TB, n), lambda i, s: (0, 0))],
            out_specs=pl.BlockSpec((1, TB, n), lambda i, s: (s[Z], 0, 0)),
        ),
    )(spot, block)


def absorb(blocks, q_places, a_places, spot, weights, wholes):
    count, with_attn = len(blocks), bool(a_places)
    width, cols = weights.shape
    attn_cols = blocks[0].shape[1] - 2 * cols
    at = lambda places, i, s: lax.rem(s[Z] + NZ + jnp.where(i == 0, places[0], places[-1]), NZ)
    q_spec = pl.BlockSpec((2, 1, TB, cols), lambda i, s: (0, at(q_places, i, s), 0, 0))
    share = pl.BlockSpec((1, TB, width), lambda i, s: (at(q_places, i, s), 0, 0))
    out_specs = [q_spec, share, share]
    out_shape = [jax.ShapeDtypeStruct((2, NZ, TB, cols), jnp.bfloat16)]
    out_shape += [jax.ShapeDtypeStruct((NZ, TB, width), jnp.bfloat16)] * 2
    if with_attn:
        out_specs.append(pl.BlockSpec((1, TB, attn_cols), lambda i, s: (at(a_places, i, s), 0, 0)))
        out_shape.append(jax.ShapeDtypeStruct((NZ, TB, attn_cols), jnp.bfloat16))
    operands = [*blocks, weights]
    in_specs = [pl.BlockSpec(v.shape, lambda i, s: (0, 0)) for v in operands]
    aliases = {}
    for k, whole in enumerate(wholes):
        if whole is not None:
            aliases[1 + len(operands)] = k
            operands.append(whole)
            in_specs.append(pl.BlockSpec(memory_space=pltpu.HBM))
    n_out = len(out_specs)

    def body(where_ref, *refs):
        weights_ref = refs[count]
        outs = refs[-n_out:]
        first = where_ref[CORE] == 0
        for k in range(count):

            @pl.when(pl.program_id(0) == k)
            def _():
                halves = [refs[k][:, :cols], refs[k][:, cols : 2 * cols]]
                outs[0][0, 0], outs[0][1, 0] = halves
                if with_attn:
                    outs[3][0] = refs[k][:, 2 * cols :]
                product = contract_cols(jnp.concatenate(halves), weights_ref[...]).astype(jnp.bfloat16)
                outs[1][0] = jnp.where(first, product[:TB], product[TB:])
                outs[2][0] = jnp.where(first, product[TB:], product[:TB])

    return pl.pallas_call(
        body,
        out_shape=tuple(out_shape),
        grid_spec=pltpu.PrefetchScalarGridSpec(
            num_scalar_prefetch=1, grid=(count,), in_specs=in_specs, out_specs=tuple(out_specs)
        ),
        input_output_aliases=aliases,
        compiler_params=pltpu.CompilerParams(vmem_limit_bytes=60 * 2**20),
        cost_estimate=pl.CostEstimate(
            flops=4 * count * TB * cols * width,
            bytes_accessed=2 * width * cols + 4 * count * TB * (2 * cols + attn_cols + width),
            transcendentals=0,
        ),
    )(spot, *operands)


def chip_parts(kept, sent, spot):
    n = kept.shape[2]
    count = NX
    hops = lambda i: jnp.where(i < 2, i, NX + 1 - i)
    pair = pl.BlockSpec((2, TB, n), lambda i, s: (lax.rem(s[X] + hops(i), NX), 0, 0))

    def body(where_ref, kept_ref, sent_ref, *outs):
        total = (kept_ref[...].astype(jnp.float32) + sent_ref[...].astype(jnp.float32)).astype(jnp.bfloat16)
        for k in range(count):

            @pl.when(pl.program_id(0) == k)
            def _():
                outs[k][...] = total.reshape(2 * TB, n)

    return pl.pallas_call(
        body,
        out_shape=(jax.ShapeDtypeStruct((2 * TB, n), jnp.bfloat16),) * count,
        grid_spec=pltpu.PrefetchScalarGridSpec(
            num_scalar_prefetch=1,
            grid=(count,),
            in_specs=[pair, pair],
            out_specs=(pl.BlockSpec((2 * TB, n), lambda i, s: (0, 0)),) * count,
        ),
        cost_estimate=pl.CostEstimate(flops=NZ * TB * n, bytes_accessed=6 * NZ * TB * n, transcendentals=0),
    )(spot, kept, sent)


def contract_rows(halves, turn, both, halves_left, factor, tile, spot):
    a, b = halves[0].shape[2], both.shape[1]
    m, n = (a, b) if halves_left else (b, a)
    half_tile, both_tile = (tile, b) if halves_left else (a, tile)
    if halves_left:
        moving = (lambda i, s: (0, 0, i), lambda i, s: (0, 0, 0, 0))
    else:
        moving = (lambda i, s: (0, 0, 0), lambda i, s: (0, 0, 0, i))

    def body(where_ref, *refs):
        both_ref, out_ref = refs[-2:]
        first = where_ref[YH] if turn else 0
        total = jnp.zeros(out_ref.shape, jnp.float32)
        parts = [ref[k] for ref in refs[:-2] for k in range(ref.shape[0])]
        for part, h in zip(parts, (first, 1 - first)):
            tokens = both_ref[:, h].reshape(NZ * TB, both_tile)
            pair = (part, tokens) if halves_left else (tokens, part)
            total += lax.dot_general(*pair, (((0,), (0,)), ((), ())), preferred_element_type=jnp.float32)
        out_ref[...] = total * factor

    return pl.pallas_call(
        body,
        out_shape=jax.ShapeDtypeStruct((m, n), jnp.float32),
        grid_spec=pltpu.PrefetchScalarGridSpec(
            num_scalar_prefetch=1,
            grid=(m // tile,),
            in_specs=[pl.BlockSpec((v.shape[0], NZ * TB, half_tile), moving[0]) for v in halves]
            + [pl.BlockSpec((NZ, 2, TB, both_tile), moving[1])],
            out_specs=pl.BlockSpec((tile, n), lambda i, s: (i, 0)),
        ),
        compiler_params=pltpu.CompilerParams(vmem_limit_bytes=40 * 2**20),
        cost_estimate=pl.CostEstimate(
            flops=4 * NZ * TB * m * n, bytes_accessed=4 * NZ * TB * (m + n) + 4 * m * n, transcendentals=0
        ),
    )(spot, *halves, both.reshape(NZ, 2, TB, b))


def contract_cols(left, right):
    return lax.dot_general(
        left, right, (((1,), (1,)), ((), ())), preferred_element_type=jnp.float32
    )


class Fold:
    def __init__(self, partial, z):
        self.partial, self.z = partial, z
        self.rows = partial.shape[0] // NZ
        self.up = self.down = None
        self.k = 4

    def mine(self, at):
        return lax.dynamic_slice_in_dim(self.partial, at % NZ * self.rows, self.rows, 0).astype(jnp.float32)

    def add(self, part, got):
        return (part if got is None else part + got.astype(jnp.float32)).astype(jnp.bfloat16)

    def step(self):
        k = self.k
        self.k -= 1
        if k < 4:
            self.up = over_z(self.add(self.mine(self.z + k), self.up), 1)
        self.down = over_z(self.add(self.mine(self.z - k + NZ), self.down), -1)

    def sums(self):
        return self.mine(self.z) + self.up.astype(jnp.float32) + self.down.astype(jnp.float32)


def shards(inputs, out_grad, attn_out, qkv_grad, w_qkv, w_out, doc_ids):
    d, t = lax.axis_index("dp"), lax.axis_index("tensor")
    z, yh = d // 2, d % 2
    x, yl, core = t // 4, t // 2 % 2, t % 2
    spot = jnp.stack([z, yh, x, core, t]).astype(jnp.int32)
    factor = 1.0 / math.sqrt(NZ * 2 * TB)

    g_all = lax.all_gather(out_grad, "tensor", axis=0, tiled=True)
    x_all = lax.all_gather(inputs, "tensor", axis=0, tiled=True)

    ids = doc_ids[None, :]
    other_ids = over_yh(ids)
    q_other = over_yh(qkv_grad)
    pair_ids = jnp.where(yh == 1, jnp.concatenate([other_ids, ids]), jnp.concatenate([ids, other_ids]))
    near = [over_z(pair_ids, 1), over_z(pair_ids, 2)]
    attn, _ = tie(attn_out, pair_ids)
    up_attn, down_attn = over_z(attn, 1), over_z(attn, -1)
    far = over_z(jnp.concatenate(near), 2)
    window = jnp.concatenate([pair_ids, *near, far]).reshape(-1)
    tables = rotary_tables(pair_ids.reshape(-1), window, z)

    up0, down0 = unrotate(qkv_grad, q_other, tables, up_attn, down_attn, spot)
    up1, down1 = tie(over_z(up0, 1), over_z(down0, -1))

    attn_all = place_first(attn_out, spot)
    *shares, attn_all = absorb([up0, down0], [0, 0], [-1, 1], spot, w_qkv, [None, None, None, attn_all])
    *shares, attn_all = absorb([up1, down1], [-1, 1], [-2, 2], spot, w_qkv, [*shares, attn_all])
    up2, down2, attn_all, *shares = tie(over_z(up1, 1), over_z(down1, -1), attn_all, *shares)

    *shares, attn_all = absorb([up2, down2], [-2, 2], [-3, 3], spot, w_qkv, [*shares, attn_all])
    attn_part = contract_cols(g_all, w_out).astype(jnp.bfloat16)
    up3, down3, attn_part, attn_all, *shares = tie(over_z(up2, 1), over_z(down2, -1), attn_part, attn_all, *shares)

    fold = Fold(attn_part, z)
    fold.step()
    last = over_z(up3[:, : 2 * qkv_grad.shape[1]], 1)
    *shares, attn_all = absorb([up3, down3], [-3, 3], [4, 4], spot, w_qkv, [*shares, attn_all])
    last, fold.down, attn_all, *shares = tie(last, fold.down, attn_all, *shares)
    q_all, kept, given = absorb([last], [4], None, spot, w_qkv, shares)

    q_all = q_all.reshape(2, NZ * TB, -1)
    sent = over_core(given)
    fold.step()
    mine, ahead, behind, across = chip_parts(kept, sent, spot)
    fold.up, fold.down, x_all, _ = tie(fold.up, fold.down, x_all, mine)
    attn_all = attn_all.reshape(1, NZ * TB, -1)
    attn_other = over_yh(attn_all)
    fold.step()
    a, b = over_x(across[:TB], 1), over_x(across[TB:], -1)
    plus = lambda part, got: (part.astype(jnp.float32) + got.astype(jnp.float32)).astype(jnp.bfloat16)
    ahead = jnp.concatenate([plus(ahead[:TB], a), ahead[TB:]])
    behind = jnp.concatenate([behind[:TB], plus(behind[TB:], b)])
    ahead, behind = tie(ahead, behind)
    x_all, _ = tie(x_all, ahead)
    wqkv_grad = contract_rows([q_all], False, x_all, False, factor, 256, spot)
    came1, came2 = over_x(ahead, 1), over_x(behind, -1)
    total = mine.astype(jnp.float32) + came1.astype(jnp.float32) + came2.astype(jnp.float32)
    keep = lax.dynamic_slice_in_dim(total, yl * TB, TB, 0)
    give = lax.dynamic_slice_in_dim(total, (1 - yl) * TB, TB, 0).astype(jnp.bfloat16)
    summed = keep + over_yl(give).astype(jnp.float32)
    input_grad = (out_grad.astype(jnp.float32) + summed).astype(jnp.bfloat16)

    fold.up, fold.down, _ = tie(fold.up, fold.down, ahead)
    fold.step()
    fold.up, fold.down, wqkv_grad = tie(fold.up, fold.down, wqkv_grad)
    sums = fold.sums()
    keep = lax.dynamic_slice_in_dim(sums, yh * TB, TB, 0)
    send = lax.dynamic_slice_in_dim(sums, (1 - yh) * TB, TB, 0).astype(jnp.bfloat16)
    attn_grad = (keep + over_yh(send).astype(jnp.float32)).astype(jnp.bfloat16)

    attn_other, _, _ = tie(attn_other, give, send)
    wout_grad = contract_rows([attn_all, attn_other], True, g_all, True, factor, 256, spot)
    return (input_grad, attn_grad, wqkv_grad, wout_grad)


def solution(mesh):
    return jax.shard_map(
        shards,
        mesh=mesh,
        in_specs=(
            P("tensor", "dp"),
            P("tensor", "dp"),
            P("dp", "tensor"),
            P("dp", "tensor"),
            P("dp", "tensor"),
            P("tensor", "dp"),
            P("dp"),
        ),
        out_specs=(P("tensor", "dp"), P("dp", "tensor"), P("dp", "tensor"), P("tensor", "dp")),
        check_vma=False,
    )
```

```python
import math

import jax
import jax.numpy as jnp
from jax import lax
from jax.experimental import pallas as pl
from jax.experimental.pallas import tpu as pltpu
from jax.sharding import PartitionSpec as P

HD = 128
HQ = 96
HK = 8
ROPE_BASE = 500000.0
NZ = 8
NX = 4
TB = 128
Z, YH, X, CORE, T = range(5)
BEHIND = 4


def over_z(value, steps):
    pairs = [(z * 2 + h, (z + steps) % NZ * 2 + h) for z in range(NZ) for h in range(2)]
    return lax.ppermute(value, "dp", pairs)


def over_yh(value):
    return lax.ppermute(value, "dp", [(d, d ^ 1) for d in range(16)])


def over_x(value, steps):
    pairs = [(x * 4 + k, (x + steps) % NX * 4 + k) for x in range(NX) for k in range(4)]
    return lax.ppermute(value, "tensor", pairs)


def over_yl(value):
    return lax.ppermute(value, "tensor", [(t, t ^ 2) for t in range(16)])


def over_core(value):
    return lax.ppermute(value, "tensor", [(t, t ^ 1) for t in range(16)])


def tie(*values):
    return lax.optimization_barrier(values)


def rotary_tables(ids, window, z):
    smaller = jnp.sum((window[None, :] < ids[:, None]).astype(jnp.int32), axis=1)
    start = jnp.maximum((z - BEHIND) * 2 * TB, 0) + smaller
    positions = z * 2 * TB + jnp.arange(2 * TB, dtype=jnp.int32) - start
    lane = jnp.arange(HD, dtype=jnp.int32)
    frequency = jnp.power(jnp.float32(ROPE_BASE), -(2.0 * (lane // 2).astype(jnp.float32)) / HD)
    angles = positions.astype(jnp.float32)[:, None] * frequency[None, :]
    sign = jnp.where(lane % 2 == 0, 1.0, -1.0)
    return jnp.cos(angles), jnp.sin(angles) * sign[None, :]


def unrotate_kernel(where_ref, own_ref, other_ref, cos_ref, sin_ref, up_attn_ref, down_attn_ref, up_ref, down_ref):
    even = lax.broadcasted_iota(jnp.int32, (TB, HD), 1) % 2 == 0
    swapped = where_ref[YH] == 1
    cols = own_ref.shape[1]
    for h in range(cols // HD):
        part = slice(h * HD, (h + 1) * HD)
        rotated = where_ref[T] * (cols // HD) + h < HQ + HK
        own, other = own_ref[:, part], other_ref[:, part]
        for half in range(2):
            rows = slice(half * TB, (half + 1) * TB)
            values = jnp.where(swapped, *((other, own) if half == 0 else (own, other))).astype(jnp.float32)
            partner = jnp.where(even, pltpu.roll(values, HD - 1, 1), pltpu.roll(values, 1, 1))
            cosine = jnp.where(rotated, cos_ref[rows, :], 1.0)
            sine = jnp.where(rotated, sin_ref[rows, :], 0.0)
            result = (values * cosine + partner * sine).astype(jnp.bfloat16)
            at = slice(half * cols + h * HD, half * cols + (h + 1) * HD)
            up_ref[:, at] = result
            down_ref[:, at] = result
    up_ref[:, 2 * cols :] = up_attn_ref[...]
    down_ref[:, 2 * cols :] = down_attn_ref[...]


def unrotate(own, other, tables, up_attn, down_attn, spot):
    cols = own.shape[1]
    vmem = pl.BlockSpec(memory_space=pltpu.VMEM)
    shape = jax.ShapeDtypeStruct((TB, 2 * cols + up_attn.shape[1]), jnp.bfloat16)
    return pl.pallas_call(
        unrotate_kernel,
        out_shape=(shape, shape),
        in_specs=[pl.BlockSpec(memory_space=pltpu.SMEM)] + [vmem] * 6,
        out_specs=(vmem, vmem),
        cost_estimate=pl.CostEstimate(flops=20 * TB * cols, bytes_accessed=16 * TB * cols, transcendentals=0),
    )(spot, own, other, *tables, up_attn, down_attn)


def place_first(block, spot):
    def body(z_ref, block_ref, out_ref):
        out_ref[0] = block_ref[...]

    n = block.shape[1]
    return pl.pallas_call(
        body,
        out_shape=jax.ShapeDtypeStruct((NZ, TB, n), jnp.bfloat16),
        grid_spec=pltpu.PrefetchScalarGridSpec(
            num_scalar_prefetch=1,
            grid=(1,),
            in_specs=[pl.BlockSpec((TB, n), lambda i, s: (0, 0))],
            out_specs=pl.BlockSpec((1, TB, n), lambda i, s: (s[Z], 0, 0)),
        ),
    )(spot, block)


def absorb(blocks, q_places, a_places, spot, weights, wholes):
    count, with_attn = len(blocks), bool(a_places)
    width, cols = weights.shape
    attn_cols = blocks[0].shape[1] - 2 * cols
    at = lambda places, i, s: lax.rem(s[Z] + NZ + jnp.where(i == 0, places[0], places[-1]), NZ)
    q_spec = pl.BlockSpec((2, 1, TB, cols), lambda i, s: (0, at(q_places, i, s), 0, 0))
    share = pl.BlockSpec((1, TB, width), lambda i, s: (at(q_places, i, s), 0, 0))
    out_specs = [q_spec, share, share]
    out_shape = [jax.ShapeDtypeStruct((2, NZ, TB, cols), jnp.bfloat16)]
    out_shape += [jax.ShapeDtypeStruct((NZ, TB, width), jnp.bfloat16)] * 2
    if with_attn:
        out_specs.append(pl.BlockSpec((1, TB, attn_cols), lambda i, s: (at(a_places, i, s), 0, 0)))
        out_shape.append(jax.ShapeDtypeStruct((NZ, TB, attn_cols), jnp.bfloat16))
    operands = [*blocks, weights]
    in_specs = [pl.BlockSpec(v.shape, lambda i, s: (0, 0)) for v in operands]
    aliases = {}
    for k, whole in enumerate(wholes):
        if whole is not None:
            aliases[1 + len(operands)] = k
            operands.append(whole)
            in_specs.append(pl.BlockSpec(memory_space=pltpu.HBM))
    n_out = len(out_specs)

    def body(where_ref, *refs):
        weights_ref = refs[count]
        outs = refs[-n_out:]
        first = where_ref[CORE] == 0
        for k in range(count):

            @pl.when(pl.program_id(0) == k)
            def _():
                halves = [refs[k][:, :cols], refs[k][:, cols : 2 * cols]]
                outs[0][0, 0], outs[0][1, 0] = halves
                if with_attn:
                    outs[3][0] = refs[k][:, 2 * cols :]
                product = contract_cols(jnp.concatenate(halves), weights_ref[...]).astype(jnp.bfloat16)
                outs[1][0] = jnp.where(first, product[:TB], product[TB:])
                outs[2][0] = jnp.where(first, product[TB:], product[:TB])

    return pl.pallas_call(
        body,
        out_shape=tuple(out_shape),
        grid_spec=pltpu.PrefetchScalarGridSpec(
            num_scalar_prefetch=1, grid=(count,), in_specs=in_specs, out_specs=tuple(out_specs)
        ),
        input_output_aliases=aliases,
        compiler_params=pltpu.CompilerParams(vmem_limit_bytes=60 * 2**20),
        cost_estimate=pl.CostEstimate(
            flops=4 * count * TB * cols * width,
            bytes_accessed=2 * width * cols + 4 * count * TB * (2 * cols + attn_cols + width),
            transcendentals=0,
        ),
    )(spot, *operands)


def chip_parts(kept, sent, spot):
    n = kept.shape[2]
    count = NX
    hops = lambda i: jnp.where(i < 2, i, NX + 1 - i)
    pair = pl.BlockSpec((2, TB, n), lambda i, s: (lax.rem(s[X] + hops(i), NX), 0, 0))

    def body(where_ref, kept_ref, sent_ref, *outs):
        total = (kept_ref[...].astype(jnp.float32) + sent_ref[...].astype(jnp.float32)).astype(jnp.bfloat16)
        for k in range(count):

            @pl.when(pl.program_id(0) == k)
            def _():
                outs[k][...] = total.reshape(2 * TB, n)

    return pl.pallas_call(
        body,
        out_shape=(jax.ShapeDtypeStruct((2 * TB, n), jnp.bfloat16),) * count,
        grid_spec=pltpu.PrefetchScalarGridSpec(
            num_scalar_prefetch=1,
            grid=(count,),
            in_specs=[pair, pair],
            out_specs=(pl.BlockSpec((2 * TB, n), lambda i, s: (0, 0)),) * count,
        ),
        cost_estimate=pl.CostEstimate(flops=NZ * TB * n, bytes_accessed=6 * NZ * TB * n, transcendentals=0),
    )(spot, kept, sent)


def contract_rows(halves, turn, both, halves_left, factor, tile, spot):
    a, b = halves[0].shape[2], both.shape[1]
    m, n = (a, b) if halves_left else (b, a)
    half_tile, both_tile = (tile, b) if halves_left else (a, tile)
    if halves_left:
        moving = (lambda i, s: (0, 0, i), lambda i, s: (0, 0, 0, 0))
    else:
        moving = (lambda i, s: (0, 0, 0), lambda i, s: (0, 0, 0, i))

    def body(where_ref, *refs):
        both_ref, out_ref = refs[-2:]
        first = where_ref[YH] if turn else 0
        total = jnp.zeros(out_ref.shape, jnp.float32)
        parts = [ref[k] for ref in refs[:-2] for k in range(ref.shape[0])]
        for part, h in zip(parts, (first, 1 - first)):
            tokens = both_ref[:, h].reshape(NZ * TB, both_tile)
            pair = (part, tokens) if halves_left else (tokens, part)
            total += lax.dot_general(*pair, (((0,), (0,)), ((), ())), preferred_element_type=jnp.float32)
        out_ref[...] = total * factor

    return pl.pallas_call(
        body,
        out_shape=jax.ShapeDtypeStruct((m, n), jnp.float32),
        grid_spec=pltpu.PrefetchScalarGridSpec(
            num_scalar_prefetch=1,
            grid=(m // tile,),
            in_specs=[pl.BlockSpec((v.shape[0], NZ * TB, half_tile), moving[0]) for v in halves]
            + [pl.BlockSpec((NZ, 2, TB, both_tile), moving[1])],
            out_specs=pl.BlockSpec((tile, n), lambda i, s: (i, 0)),
        ),
        compiler_params=pltpu.CompilerParams(vmem_limit_bytes=(40 if turn else 60) * 2**20),
        cost_estimate=pl.CostEstimate(
            flops=4 * NZ * TB * m * n, bytes_accessed=4 * NZ * TB * (m + n) + 4 * m * n, transcendentals=0
        ),
    )(spot, *halves, both.reshape(NZ, 2, TB, b))


def contract_cols(left, right):
    return lax.dot_general(
        left, right, (((1,), (1,)), ((), ())), preferred_element_type=jnp.float32
    )


class Fold:
    def __init__(self, partial, z):
        self.partial, self.z = partial, z
        self.rows = partial.shape[0] // NZ
        self.up = self.down = None
        self.k = 4

    def mine(self, at):
        return lax.dynamic_slice_in_dim(self.partial, at % NZ * self.rows, self.rows, 0).astype(jnp.float32)

    def add(self, part, got):
        return (part if got is None else part + got.astype(jnp.float32)).astype(jnp.bfloat16)

    def step(self):
        k = self.k
        self.k -= 1
        if k < 4:
            self.up = over_z(self.add(self.mine(self.z + k), self.up), 1)
        self.down = over_z(self.add(self.mine(self.z - k + NZ), self.down), -1)

    def sums(self):
        return self.mine(self.z) + self.up.astype(jnp.float32) + self.down.astype(jnp.float32)


def shards(inputs, out_grad, attn_out, qkv_grad, w_qkv, w_out, doc_ids):
    d, t = lax.axis_index("dp"), lax.axis_index("tensor")
    z, yh = d // 2, d % 2
    x, yl, core = t // 4, t // 2 % 2, t % 2
    spot = jnp.stack([z, yh, x, core, t]).astype(jnp.int32)
    factor = 1.0 / math.sqrt(NZ * 2 * TB)

    g_all = lax.all_gather(out_grad, "tensor", axis=0, tiled=True)
    x_all = lax.all_gather(inputs, "tensor", axis=0, tiled=True)

    ids = doc_ids[None, :]
    other_ids = over_yh(ids)
    q_other = over_yh(qkv_grad)
    pair_ids = jnp.where(yh == 1, jnp.concatenate([other_ids, ids]), jnp.concatenate([ids, other_ids]))
    near = [over_z(pair_ids, 1), over_z(pair_ids, 2)]
    attn, _ = tie(attn_out, pair_ids)
    up_attn, down_attn = over_z(attn, 1), over_z(attn, -1)
    far = over_z(jnp.concatenate(near), 2)
    window = jnp.concatenate([pair_ids, *near, far]).reshape(-1)
    tables = rotary_tables(pair_ids.reshape(-1), window, z)

    up0, down0 = unrotate(qkv_grad, q_other, tables, up_attn, down_attn, spot)
    up1, down1 = tie(over_z(up0, 1), over_z(down0, -1))

    attn_all = place_first(attn_out, spot)
    *shares, attn_all = absorb([up0, down0], [0, 0], [-1, 1], spot, w_qkv, [None, None, None, attn_all])
    *shares, attn_all = absorb([up1, down1], [-1, 1], [-2, 2], spot, w_qkv, [*shares, attn_all])
    up2, down2, attn_all, *shares = tie(over_z(up1, 1), over_z(down1, -1), attn_all, *shares)

    *shares, attn_all = absorb([up2, down2], [-2, 2], [-3, 3], spot, w_qkv, [*shares, attn_all])
    attn_part = contract_cols(g_all, w_out).astype(jnp.bfloat16)
    up3, down3, attn_part, attn_all, *shares = tie(over_z(up2, 1), over_z(down2, -1), attn_part, attn_all, *shares)

    fold = Fold(attn_part, z)
    fold.step()
    last = over_z(up3[:, : 2 * qkv_grad.shape[1]], 1)
    *shares, attn_all = absorb([up3, down3], [-3, 3], [4, 4], spot, w_qkv, [*shares, attn_all])
    last, fold.down, attn_all, *shares = tie(last, fold.down, attn_all, *shares)
    q_all, kept, given = absorb([last], [4], None, spot, w_qkv, shares)

    q_all = q_all.reshape(2, NZ * TB, -1)
    sent = over_core(given)
    fold.step()
    mine, ahead, behind, across = chip_parts(kept, sent, spot)
    fold.up, fold.down, x_all, _ = tie(fold.up, fold.down, x_all, mine)
    attn_all = attn_all.reshape(1, NZ * TB, -1)
    attn_other = over_yh(attn_all)
    fold.step()
    a, b = over_x(across[:TB], 1), over_x(across[TB:], -1)
    plus = lambda part, got: (part.astype(jnp.float32) + got.astype(jnp.float32)).astype(jnp.bfloat16)
    ahead = jnp.concatenate([plus(ahead[:TB], a), ahead[TB:]])
    behind = jnp.concatenate([behind[:TB], plus(behind[TB:], b)])
    ahead, behind = tie(ahead, behind)
    x_all, _ = tie(x_all, ahead)
    wqkv_grad = contract_rows([q_all], False, x_all, False, factor, 256, spot)
    came1, came2 = over_x(ahead, 1), over_x(behind, -1)
    total = mine.astype(jnp.float32) + came1.astype(jnp.float32) + came2.astype(jnp.float32)
    keep = lax.dynamic_slice_in_dim(total, yl * TB, TB, 0)
    give = lax.dynamic_slice_in_dim(total, (1 - yl) * TB, TB, 0).astype(jnp.bfloat16)
    summed = keep + over_yl(give).astype(jnp.float32)
    input_grad = (out_grad.astype(jnp.float32) + summed).astype(jnp.bfloat16)

    fold.up, fold.down, _ = tie(fold.up, fold.down, ahead)
    fold.step()
    fold.up, fold.down, wqkv_grad = tie(fold.up, fold.down, wqkv_grad)
    sums = fold.sums()
    keep = lax.dynamic_slice_in_dim(sums, yh * TB, TB, 0)
    send = lax.dynamic_slice_in_dim(sums, (1 - yh) * TB, TB, 0).astype(jnp.bfloat16)
    attn_grad = (keep + over_yh(send).astype(jnp.float32)).astype(jnp.bfloat16)

    attn_other, _, _ = tie(attn_other, give, send)
    wout_grad = contract_rows([attn_all, attn_other], True, g_all, True, factor, 256, spot)
    return (input_grad, attn_grad, wqkv_grad, wout_grad)


def solution(mesh):
    return jax.shard_map(
        shards,
        mesh=mesh,
        in_specs=(
            P("tensor", "dp"),
            P("tensor", "dp"),
            P("dp", "tensor"),
            P("dp", "tensor"),
            P("dp", "tensor"),
            P("tensor", "dp"),
            P("dp"),
        ),
        out_specs=(P("tensor", "dp"), P("dp", "tensor"), P("dp", "tensor"), P("tensor", "dp")),
        check_vma=False,
    )
```
